32 devices in a mesh: fibre: 8 (over y, x, core), tm: 4 (over z).
Axes of the slice: x: 2, y: 2, z: 4, core: 2. Of those that a mesh axis runs over, the one named last changes fastest.
Arguments:
- traces: float32 [1024, 32, 512], P('fibre', 'tm'), may hold values from -6 to 6
Outputs:
- correlations: float32 [1024, 32, 256], P(('fibre', 'tm'))
The draws below stay inside these ranges and needn't reach their ends.
All inputs are finite; a program needn't handle non-finite values.
Results may differ from the reference program's by a relative error of at most 0.0003.
Values sent between devices are 32-bit elements; how exact they have to be, the bound alone decides.
No kernel may reach another device: no remote copies, remote signals or barrier semaphores. Data moves between devices by JAX's collectives and lax.ppermute only.
A program may use at most 128 MiB of HBM per device.

```python
import math
import jax
import jax.numpy as jnp
from jax import lax

CH_DEV = 128
NEAR = 32
WIN = 512
BINS = 256
LAGS = 256
HALF = 8
CHANNELS = 1024
SEGS = 32


def level_of(rng, dims, pieces, low, top_value):
    factor_of, own = 1.0, jax.random.fold_in(rng, 6)
    for position, parts in pieces:
        draws = jnp.exp(jax.random.uniform(jax.random.fold_in(own, position), (parts,), jnp.float32, low / len(pieces), top_value / len(pieces)))
        factor_of = factor_of * jnp.repeat(draws, dims[position] // parts).reshape([-1 if axis == position else 1 for axis in range(len(dims))])
    return factor_of


def normal_values(rng, shape, deviation, most, pieces=(), kind=jnp.bfloat16):
    array = jax.random.normal(rng, shape, jnp.float32) * deviation
    if len(pieces) > 0:
        array = level_of(rng, shape, pieces, -0.22, 0.18) * array
    return jnp.clip(array, min=-most, max=most).astype(kind)


def setup_inputs(seed: int = 0) -> dict:
    seeds = jax.random.split(jax.random.key(seed), 2)
    traces = normal_values(seeds[0], (CHANNELS, SEGS, WIN), 1.0, 6.0, ((0, 8), (1, 4)), jnp.float32)
    return {"traces": traces}


def make_tables(win, bins, lags, segs):
    sample_idx = jnp.arange(win, dtype=jnp.int32)[:, None]
    bin_idx = jnp.arange(1, bins + 1, dtype=jnp.int32)[None, :]
    phases = (sample_idx * bin_idx % win).astype(jnp.float32) * (2.0 * math.pi / win)
    hann_taper = 0.5 - 0.5 * jnp.cos(sample_idx.astype(jnp.float32) * (2.0 * math.pi / win))
    forward = jnp.concatenate([hann_taper * jnp.cos(phases), -hann_taper * jnp.sin(phases)], axis=1)
    rows_idx = jnp.arange(bins, dtype=jnp.int32)
    band_matrix = (jnp.abs(rows_idx[:, None] - rows_idx[None, :]) <= HALF).astype(jnp.float32) / (2 * HALF + 1)
    lag_shift = jnp.arange(lags, dtype=jnp.int32)[None, :] - lags // 2
    back_phase = (bin_idx.reshape(bins, 1) * lag_shift % win).astype(jnp.float32) * (2.0 * math.pi / win)
    inverse = jnp.concatenate([jnp.cos(back_phase), -jnp.sin(back_phase)], axis=0) / segs
    return (forward, band_matrix, inverse)

def whiten(samples, forward, band_matrix):
    channels, segments, win = samples.shape
    bins = forward.shape[1] // 2
    seg_rows = samples.reshape(channels * segments, win)
    spectrum = jnp.dot(seg_rows, forward, precision=lax.Precision.HIGHEST)
    real_part = spectrum[:, :bins]
    imag_part = spectrum[:, bins:]
    energy = real_part * real_part + imag_part * imag_part
    smoothed = jnp.dot(energy, band_matrix, precision=lax.Precision.HIGHEST)
    overall = lax.optimization_barrier(jnp.mean(energy, axis=1, keepdims=True))
    divisor = jnp.sqrt(smoothed + 0.1 * overall + 1e-06)
    whitened = jnp.concatenate([real_part / divisor, imag_part / divisor], axis=1)
    return whitened.reshape(channels, segments, 2 * bins)

def reference(traces):
    forward, band_matrix, inverse = make_tables(WIN, BINS, LAGS, SEGS)
    padded = jnp.pad(traces, ((0, NEAR), (0, 0), (0, 0)))

    def one_block(block_id):
        start = (block_id * CH_DEV).astype(jnp.int32)
        window = lax.dynamic_slice(padded, (start, jnp.int32(0), jnp.int32(0)), (CH_DEV + NEAR, SEGS, WIN))
        spectra = whiten(window, forward, band_matrix)
        own = spectra[:CH_DEV]
        own_re = own[..., :BINS]
        own_im = own[..., BINS:]
        real_terms = []
        imag_terms = []
        for offset in range(1, NEAR + 1):
            other = spectra[offset:offset + CH_DEV]
            other_re = other[..., :BINS]
            other_im = other[..., BINS:]
            real_terms.append(lax.optimization_barrier(jnp.sum(own_re * other_re + own_im * other_im, axis=1)))
            imag_terms.append(lax.optimization_barrier(jnp.sum(own_im * other_re - own_re * other_im, axis=1)))
        pairs = jnp.concatenate([jnp.stack(real_terms, axis=1), jnp.stack(imag_terms, axis=1)], axis=2)
        lagged = jnp.dot(pairs.reshape(CH_DEV * NEAR, 2 * BINS), inverse, precision=lax.Precision.HIGHEST)
        return lagged.reshape(CH_DEV, NEAR, LAGS)
    blocks = lax.map(one_block, jnp.arange(CHANNELS // CH_DEV, dtype=jnp.int32))
    return blocks.reshape(CHANNELS, NEAR, LAGS)
```

```python
import functools

import jax
import jax.numpy as jnp
import ml_dtypes
import numpy as np
from jax import lax
from jax.experimental import pallas as pl
from jax.experimental.pallas import tpu as pltpu
from jax.sharding import PartitionSpec as P

NEAR = 32
LAGS = 256
HALF = 8
LANES = 128
VMEM_LIMIT = 48 << 20


def split_table(table):
    high = table.astype(ml_dtypes.bfloat16)
    low = (table - high.astype(np.float64)).astype(ml_dtypes.bfloat16)
    return np.stack([high, low])


def make_tables(win, lags, segs):
    bins = win // 2
    samples = np.arange(win)
    hann = 0.5 - 0.5 * np.cos(2.0 * np.pi * samples / win)
    even, odd = np.arange(2, bins + 1, 2), np.arange(1, bins, 2)
    order = np.concatenate([even, odd])

    def forward(picked):
        phases = 2.0 * np.pi * ((samples[: win // 2, None] * picked[None, :]) % win) / win
        return split_table(np.concatenate([np.cos(phases), -np.sin(phases)], axis=1))

    near = np.abs(order[:, None] - order[None, :]) <= HALF
    band = near / (2.0 * HALF + 1.0) + 0.1 / bins
    lag = np.arange(lags) - lags // 2
    phases = 2.0 * np.pi * ((order[:, None] * lag[None, :]) % win) / win
    inverse = np.concatenate([np.cos(phases), -np.sin(phases)], axis=0) / segs
    return {
        "hann": hann.astype(np.float32)[None, :],
        "even": forward(even),
        "odd": forward(odd),
        "band": split_table(band),
        "inverse": split_table(inverse),
    }


def dot_split(value, table):
    high = value.astype(jnp.bfloat16)
    low = (value - high.astype(jnp.float32)).astype(jnp.bfloat16)
    dot = functools.partial(jnp.dot, preferred_element_type=jnp.float32)
    return dot(high, table[0]) + (dot(high, table[1]) + dot(low, table[0]))


def whiten_kernel(x_ref, hann, even, odd, band, w_ref, stage):
    channels, segs, win = x_ref.shape
    parts = win // LANES
    for part in range(parts):
        lanes = slice(LANES * part, LANES * part + LANES)
        stage[part] = x_ref[:, :, lanes].reshape(channels * segs, LANES)
    pieces = []
    for s in range(segs):
        pieces.append([
            stage[part, pl.ds(s, channels, stride=segs), :] * hann[:, LANES * part : LANES * part + LANES]
            for part in range(parts)
        ])
    quarter = [jnp.concatenate([piece[part] for piece in pieces], axis=0) for part in range(parts)]
    both = jnp.concatenate([quarter[0] + quarter[2], quarter[1] + quarter[3]], axis=1)
    between = jnp.concatenate([quarter[0] - quarter[2], quarter[1] - quarter[3]], axis=1)
    spectra = (dot_split(both, even), dot_split(between, odd))
    energy = jnp.concatenate(
        [sp[:, :LANES] * sp[:, :LANES] + sp[:, LANES:] * sp[:, LANES:] for sp in spectra], axis=1
    )
    scale = lax.rsqrt(dot_split(energy, band) + 1e-06)
    for half, sp in enumerate(spectra):
        own = scale[:, LANES * half : LANES * half + LANES]
        real, imag = sp[:, :LANES] * own, sp[:, LANES:] * own
        for s in range(segs):
            rows = slice(channels * s, channels * s + channels)
            w_ref[half, 0, s] = real[rows]
            w_ref[half, 1, s] = imag[rows]


def whiten(x, tables):
    blocks, near, segs, win = x.shape
    whole = lambda a: pl.BlockSpec(a.shape, lambda i: (0,) * a.ndim)
    names = ("hann", "even", "odd", "band")
    consts = [jnp.asarray(tables[name]) for name in names]
    return pl.pallas_call(
        whiten_kernel,
        grid=(blocks,),
        in_specs=[pl.BlockSpec((None, near, segs, win), lambda i: (i, 0, 0, 0))] + [whole(c) for c in consts],
        out_specs=pl.BlockSpec((None, 2, 2, segs, near, LANES), lambda i: (i, 0, 0, 0, 0, 0)),
        out_shape=jax.ShapeDtypeStruct((blocks, 2, 2, segs, near, LANES), jnp.float32),
        scratch_shapes=[pltpu.VMEM((win // LANES, near * segs, LANES), jnp.float32)],
        compiler_params=pltpu.CompilerParams(vmem_limit_bytes=VMEM_LIMIT),
        cost_estimate=pl.CostEstimate(flops=blocks * 500_000_000, bytes_accessed=blocks << 20, transcendentals=0),
        name="whiten",
    )(x, *consts)


def cross_kernel(count, first, pick_ref, *refs):
    cands = refs[: 2 * count]
    rest = refs[2 * count :]
    prior, (acc, pair) = (None, rest) if first else (rest[0], rest[1:])
    _, segs, near, _ = cands[0].shape
    for side in range(2):
        for part in range(2):
            for s in range(segs):
                value = cands[side * count][part, s]
                for other in range(1, count):
                    value = jnp.where(pick_ref[0] == other, cands[side * count + other][part, s], value)
                pair[part, s, pl.ds(side * near, near), :] = value
    for group in range(near // 8):
        rows = pl.ds(8 * group, 8)
        real = [pair[0, s, rows, :] for s in range(segs)]
        imag = [pair[1, s, rows, :] for s in range(segs)]
        added = [real[s] + imag[s] for s in range(segs)]
        for offset in range(1, near + 1):
            ahead = pl.ds(8 * group + offset, 8)
            rr = ii = mixed = None
            for s in range(segs):
                other_re, other_im = pair[0, s, ahead, :], pair[1, s, ahead, :]
                terms = (real[s] * other_re, imag[s] * other_im, added[s] * (other_re - other_im))
                if rr is None:
                    rr, ii, mixed = terms
                else:
                    rr, ii, mixed = rr + terms[0], ii + terms[1], mixed + terms[2]
            cross_re, cross_im = rr + ii, mixed - rr + ii
            if not first:
                cross_re = cross_re + prior[0, offset - 1, rows, :]
                cross_im = cross_im + prior[1, offset - 1, rows, :]
            acc[0, offset - 1, rows, :] = cross_re
            acc[1, offset - 1, rows, :] = cross_im


def cross(pick, firsts, seconds, prior=None):
    count = len(firsts)
    halves, parts, segs, near, lanes = firsts[0].shape
    half_spec = pl.BlockSpec((None, parts, segs, near, lanes), lambda i, p: (i, 0, 0, 0, 0))
    acc_spec = pl.BlockSpec((None, 2, near, near, lanes), lambda i, p: (i, 0, 0, 0, 0))
    first = prior is None
    return pl.pallas_call(
        functools.partial(cross_kernel, count, first),
        grid_spec=pltpu.PrefetchScalarGridSpec(
            num_scalar_prefetch=1,
            grid=(halves,),
            in_specs=[half_spec] * (2 * count) + ([] if first else [acc_spec]),
            out_specs=acc_spec,
            scratch_shapes=[pltpu.VMEM((parts, segs, 2 * near, lanes), jnp.float32)],
        ),
        out_shape=jax.ShapeDtypeStruct((halves, 2, near, near, lanes), jnp.float32),
        compiler_params=pltpu.CompilerParams(vmem_limit_bytes=VMEM_LIMIT),
        cost_estimate=pl.CostEstimate(flops=4_000_000_000, bytes_accessed=4 << 20, transcendentals=0),
        name="cross",
    )(pick, *firsts, *seconds, *([] if first else [prior]))


def invert_kernel(acc, table, out_ref, stage):
    near = acc.shape[3]
    chunks = 4
    step = near // chunks
    for chunk in range(chunks):
        offsets = slice(chunk * step, chunk * step + step)
        lhs = jnp.concatenate(
            [acc[half, part, offsets].reshape(step * near, LANES) for part in range(2) for half in range(2)], axis=1
        )
        lagged = dot_split(lhs, table)
        for part in range(lagged.shape[1] // LANES):
            for j in range(step):
                stage[part, pl.ds(chunk * step + j, near, stride=near), :] = lagged[
                    near * j : near * j + near, LANES * part : LANES * part + LANES
                ]
    for part in range(stage.shape[0]):
        out_ref[:, :, LANES * part : LANES * part + LANES] = stage[part].reshape(near, near, LANES)


def invert(acc, tables):
    near = acc.shape[3]
    vmem = pl.BlockSpec(memory_space=pltpu.VMEM)
    return pl.pallas_call(
        invert_kernel,
        in_specs=[vmem, vmem],
        out_specs=vmem,
        out_shape=jax.ShapeDtypeStruct((near, near, LAGS), jnp.float32),
        scratch_shapes=[pltpu.VMEM((LAGS // LANES, near * near, LANES), jnp.float32)],
        compiler_params=pltpu.CompilerParams(vmem_limit_bytes=VMEM_LIMIT),
        cost_estimate=pl.CostEstimate(flops=2_000_000_000, bytes_accessed=3 << 20, transcendentals=0),
        name="invert",
    )(acc, jnp.asarray(tables["inverse"]))


def shifted(value, steps):
    count = lax.axis_size("fibre")
    return lax.ppermute(value, "fibre", [(source, source + steps) for source in range(max(0, -steps), count)])


def line_of_four(traces):
    channels, segs, win = traces.shape
    tables = make_tables(win, LAGS, segs * 4)
    z = lax.axis_index("tm")
    blocks = traces.reshape(4, NEAR, segs, win)
    halo = shifted(blocks[0], -1)
    own = whiten(blocks, tables)
    ahead = whiten(halo[None], tables)[0]
    own5 = jnp.concatenate([own, ahead[None]], axis=0)

    def block(at):
        return lax.dynamic_index_in_dim(own5, at, 0, keepdims=False)

    def choose(*picks):
        return block(jnp.asarray(picks, jnp.int32)[z])

    def outer(value):
        return lax.ppermute(value, "tm", [(0, 1), (3, 2)])

    def middle(value):
        return lax.ppermute(value, "tm", [(1, 2), (2, 1)])

    def inner(value):
        return lax.ppermute(value, "tm", [(1, 0), (2, 3)])

    far = choose(3, 3, 0, 0)
    farther = choose(4, 4, 1, 1)
    e1 = outer(far)
    m1 = middle(far)
    i1 = inner(choose(0, 0, 3, 3))
    e2 = outer(farther)
    m2 = middle(farther)
    i2 = inner(choose(1, 1, 4, 4))
    second = own[2]
    m3 = middle(second)
    e3 = outer(second)
    m4 = middle(e1)
    i3 = inner(m1)
    e4 = outer(choose(1, 1, 3, 3))
    m5 = middle(e2)
    i4 = inner(m2)
    m6 = middle(e3)
    i5 = inner(m4)
    i6 = inner(m5)
    role = jnp.asarray([0, 1, 2, 0], jnp.int32)[z][None]
    zero = jnp.zeros((1,), jnp.int32)
    acc = cross(zero, [block(z)], [block(z + 1)])
    acc = cross(role, [i1, e4, e3], [i2, e3, e4], acc)
    acc = cross(role, [i3, m2, m3], [i4, m3, m1], acc)
    acc = cross(role, [i5, m5, m6], [i6, m6, m4], acc)
    return invert(acc, tables)


def band_of(products):
    count, _, width = products.shape[0], products.shape[1], products.shape[2]
    flat_rows = products.reshape(count * 2 * count, width)[1:]
    flat_rows = jnp.pad(flat_rows, ((0, count + 1), (0, 0)))
    return flat_rows.reshape(count, 2 * count + 1, width)[:, :count]


def any_line(traces):
    channels, segs, win = traces.shape
    bins = win // 2
    axis = lax.axis_size("tm")
    tables = make_tables(win, LAGS, segs * axis)
    blocks = traces.reshape(channels // NEAR, NEAR, segs, win)
    halo = shifted(blocks[0], -1)
    spectra = whiten(jnp.concatenate([blocks, halo[None]], axis=0), tables)
    zero = jnp.zeros((1,), jnp.int32)
    inverse = tables["inverse"].astype(np.float32)
    inverse = jnp.asarray(inverse[0] + inverse[1])
    pieces = []
    for index in range(channels // NEAR):
        acc = cross(zero, [spectra[index]], [spectra[index + 1]])
        pairs = acc.transpose(3, 2, 1, 0, 4).reshape(NEAR * NEAR, 2 * bins)
        pieces.append(jnp.dot(pairs, inverse, precision=lax.Precision.HIGHEST))
    lagged = jnp.concatenate(pieces, axis=0).reshape(channels, NEAR, LAGS)
    return lax.psum_scatter(lagged, "tm", scatter_dimension=0, tiled=True)


def shards(traces):
    if lax.axis_size("tm") == 4 and traces.shape[0] == 4 * NEAR:
        return line_of_four(traces)
    return any_line(traces)


def solution(mesh):
    in_specs = (P("fibre", "tm", None),)
    out_specs = P(("fibre", "tm"), None, None)
    return jax.shard_map(shards, mesh=mesh, in_specs=in_specs, out_specs=out_specs, check_vma=False)
```

```python
import functools

import jax
import jax.numpy as jnp
import ml_dtypes
import numpy as np
from jax import lax
from jax.experimental import pallas as pl
from jax.experimental.pallas import tpu as pltpu
from jax.sharding import PartitionSpec as P

NEAR = 32
LAGS = 256
HALF = 8
LANES = 128
VMEM_LIMIT = 48 << 20


def split_table(table):
    high = table.astype(ml_dtypes.bfloat16)
    low = (table - high.astype(np.float64)).astype(ml_dtypes.bfloat16)
    return np.stack([high, low])


def make_tables(win, lags, segs):
    bins = win // 2
    samples = np.arange(win)
    hann = 0.5 - 0.5 * np.cos(2.0 * np.pi * samples / win)
    even, odd = np.arange(2, bins + 1, 2), np.arange(1, bins, 2)
    order = np.concatenate([even, odd])

    def forward(picked):
        phases = 2.0 * np.pi * ((samples[: win // 2, None] * picked[None, :]) % win) / win
        return split_table(np.concatenate([np.cos(phases), -np.sin(phases)], axis=1))

    near = np.abs(order[:, None] - order[None, :]) <= HALF
    band = near / (2.0 * HALF + 1.0) + 0.1 / bins
    lag = np.arange(lags) - lags // 2
    phases = 2.0 * np.pi * ((order[:, None] * lag[None, :]) % win) / win
    halves = np.split(phases, 2)
    inverse = np.stack([split_table(np.concatenate([np.cos(h), -np.sin(h)], axis=0) / segs) for h in halves])
    return {
        "hann": hann.astype(np.float32)[None, :],
        "even": forward(even),
        "odd": forward(odd),
        "band": split_table(band),
        "inverse": inverse,
    }


def dot_split(value, table):
    high = value.astype(jnp.bfloat16)
    low = (value - high.astype(jnp.float32)).astype(jnp.bfloat16)
    dot = functools.partial(jnp.dot, preferred_element_type=jnp.float32)
    return dot(high, table[0]) + (dot(high, table[1]) + dot(low, table[0]))


def whiten_kernel(x_ref, hann, even, odd, band, w_ref, stage):
    channels, segs, win = x_ref.shape
    parts = win // LANES
    for part in range(parts):
        lanes = slice(LANES * part, LANES * part + LANES)
        stage[part] = x_ref[:, :, lanes].reshape(channels * segs, LANES)
    pieces = []
    for s in range(segs):
        pieces.append([
            stage[part, pl.ds(s, channels, stride=segs), :] * hann[:, LANES * part : LANES * part + LANES]
            for part in range(parts)
        ])
    quarter = [jnp.concatenate([piece[part] for piece in pieces], axis=0) for part in range(parts)]
    both = jnp.concatenate([quarter[0] + quarter[2], quarter[1] + quarter[3]], axis=1)
    between = jnp.concatenate([quarter[0] - quarter[2], quarter[1] - quarter[3]], axis=1)
    spectra = (dot_split(both, even), dot_split(between, odd))
    energy = jnp.concatenate(
        [sp[:, :LANES] * sp[:, :LANES] + sp[:, LANES:] * sp[:, LANES:] for sp in spectra], axis=1
    )
    scale = lax.rsqrt(dot_split(energy, band) + 1e-06)
    for half, sp in enumerate(spectra):
        own = scale[:, LANES * half : LANES * half + LANES]
        real, imag = sp[:, :LANES] * own, sp[:, LANES:] * own
        for s in range(segs):
            rows = slice(channels * s, channels * s + channels)
            w_ref[half, 0, s] = real[rows]
            w_ref[half, 1, s] = imag[rows]


def whiten(x, tables):
    blocks, near, segs, win = x.shape
    whole = lambda a: pl.BlockSpec(a.shape, lambda i: (0,) * a.ndim)
    names = ("hann", "even", "odd", "band")
    consts = [jnp.asarray(tables[name]) for name in names]
    return pl.pallas_call(
        whiten_kernel,
        grid=(blocks,),
        in_specs=[pl.BlockSpec((None, near, segs, win), lambda i: (i, 0, 0, 0))] + [whole(c) for c in consts],
        out_specs=pl.BlockSpec((None, 2, 2, segs, near, LANES), lambda i: (i, 0, 0, 0, 0, 0)),
        out_shape=jax.ShapeDtypeStruct((blocks, 2, 2, segs, near, LANES), jnp.float32),
        scratch_shapes=[pltpu.VMEM((win // LANES, near * segs, LANES), jnp.float32)],
        compiler_params=pltpu.CompilerParams(vmem_limit_bytes=VMEM_LIMIT),
        cost_estimate=pl.CostEstimate(flops=blocks * 500_000_000, bytes_accessed=blocks << 20, transcendentals=0),
        name="whiten",
    )(x, *consts)


def groups_of(near, which):
    tiles = near // 8
    inside = [(tile, offset) for tile in range(tiles) for offset in range(1, near - 8 * tile - 7)]
    across = [(tile, offset) for tile in range(tiles) for offset in range(near - 8 * tile - 7, near + 1)]
    return {"inside": inside, "across": across, "all": inside + across}[which]


def products(pair, groups, store):
    segs = pair.shape[1]
    tile = None
    for index, (group, offset) in enumerate(groups):
        if group != tile:
            tile = group
            rows = pl.ds(8 * group, 8)
            real = [pair[0, s, rows, :] for s in range(segs)]
            imag = [pair[1, s, rows, :] for s in range(segs)]
            added = [real[s] + imag[s] for s in range(segs)]
        ahead = pl.ds(8 * group + offset, 8)
        rr = ii = mixed = None
        for s in range(segs):
            other_re, other_im = pair[0, s, ahead, :], pair[1, s, ahead, :]
            terms = (real[s] * other_re, imag[s] * other_im, added[s] * (other_re - other_im))
            if rr is None:
                rr, ii, mixed = terms
            else:
                rr, ii, mixed = rr + terms[0], ii + terms[1], mixed + terms[2]
        store(index, rr + ii, mixed - rr + ii)


def lag_kernel(near, which, count, has_prior, pick_ref, *refs):
    half = pl.program_id(1)
    sides = 1 if which == "inside" else 2
    cands, refs = refs[: sides * count], refs[sides * count :]
    table, refs = refs[0], refs[1:]
    sizes = {"inside": ("inside",), "across": ("across",), "all": ("inside", "across")}[which]
    priors, refs = (refs[: len(sizes)], refs[len(sizes) :]) if has_prior else (None, refs)
    outs, (pair, lhs) = refs[: len(sizes)], refs[len(sizes) :]
    segs = cands[0].shape[1]
    for side in range(sides):
        for part in range(2):
            for s in range(segs):
                value = cands[side * count][part, s]
                for other in range(1, count):
                    value = jnp.where(pick_ref[0] == other, cands[side * count + other][part, s], value)
                pair[part, s, pl.ds(side * near, near), :] = value

    def store(index, real, imag):
        lhs[pl.ds(8 * index, 8), :LANES] = real
        lhs[pl.ds(8 * index, 8), LANES:] = imag

    products(pair, groups_of(near, which), store)
    start = 0
    for index, out in enumerate(outs):
        count_rows = out.shape[0] * 8
        lagged = dot_split(lhs[pl.ds(start, count_rows), :], table).reshape(out.shape)
        start += count_rows

        @pl.when(half == 0)
        def _():
            out[...] = lagged + priors[index][...] if has_prior else lagged

        @pl.when(half != 0)
        def _():
            out[...] += lagged


def lag_sums(which, pick, firsts, seconds, tables, base=None, prior=None, blocks=1, total=1, grown=None):
    count = len(firsts)
    halves, parts, segs, near, lanes = firsts[0].shape[-5:]
    if base is None:
        spec = pl.BlockSpec((None, parts, segs, near, lanes), lambda b, h, p: (h, 0, 0, 0, 0))
        specs = [spec] * count
        specs2 = specs
    else:
        specs = [pl.BlockSpec((None, None, parts, segs, near, lanes), lambda b, h, p: (b, h, 0, 0, 0, 0))]
        specs2 = [pl.BlockSpec((None, None, parts, segs, near, lanes), lambda b, h, p: (b + 1, h, 0, 0, 0, 0))]
    operands = list(firsts)
    in_specs = list(specs)
    sides = 1
    if which != "inside":
        operands += list(seconds)
        in_specs += list(specs2)
        sides = 2
    table = tables["inverse"]
    operands.append(jnp.asarray(table))
    in_specs.append(pl.BlockSpec((None,) + table.shape[1:], lambda b, h, p: (h, 0, 0, 0)))
    kinds = {"inside": ("inside",), "across": ("across",), "all": ("inside", "across")}[which]
    shapes = [(len(groups_of(near, kind)), 8, LAGS) for kind in kinds]
    aliases = {}
    if prior is not None:
        for value, shape in zip(prior, shapes):
            operands.append(value)
            in_specs.append(pl.BlockSpec((None,) + shape, lambda b, h, p: (p[1], 0, 0, 0)))
    kernel = functools.partial(lag_kernel, near, which, count, prior is not None)
    first_block = 0
    if grown is not None:
        first_block = total - blocks
        inner = kernel

        def kernel(pick_ref, *refs):
            seen = sides * count + 1
            return inner(pick_ref, *refs[:seen], *refs[seen + len(grown) :])

        for index, value in enumerate(grown):
            aliases[1 + len(operands)] = index
            operands.append(value)
            in_specs.append(pl.BlockSpec(memory_space=pl.ANY))
    rows = 8 * sum(shape[0] for shape in shapes)
    work = blocks * rows // 8
    return pl.pallas_call(
        kernel,
        grid_spec=pltpu.PrefetchScalarGridSpec(
            num_scalar_prefetch=1,
            grid=(blocks, halves),
            in_specs=in_specs,
            out_specs=[
                pl.BlockSpec((None,) + shape, lambda b, h, p: (b + first_block, 0, 0, 0)) for shape in shapes
            ],
            scratch_shapes=[
                pltpu.VMEM((parts, segs, sides * near, lanes), jnp.float32),
                pltpu.VMEM((rows, 2 * lanes), jnp.float32),
            ],
        ),
        out_shape=[jax.ShapeDtypeStruct((total,) + shape, jnp.float32) for shape in shapes],
        input_output_aliases=aliases,
        compiler_params=pltpu.CompilerParams(vmem_limit_bytes=VMEM_LIMIT),
        cost_estimate=pl.CostEstimate(flops=work * 20_000_000, bytes_accessed=1 << 20, transcendentals=0),
        name="lag_" + which,
    )(pick, *operands)


def place_kernel(near, count, *refs):
    terms, out_ref, stage = refs[: 2 * count], refs[2 * count], refs[2 * count + 1]
    for kind in range(2):
        for index, (tile, offset) in enumerate(groups_of(near, ("inside", "across")[kind])):
            value = terms[kind * count][index]
            for other in range(1, count):
                value = value + terms[kind * count + other][index]
            for part in range(LAGS // LANES):
                stage[part, pl.ds(8 * tile * near + offset - 1, 8, stride=near), :] = value[
                    :, LANES * part : LANES * part + LANES
                ]
    for part in range(LAGS // LANES):
        out_ref[:, :, LANES * part : LANES * part + LANES] = stage[part].reshape(near, near, LANES)


def place(near, inside, across):
    vmem = pl.BlockSpec(memory_space=pltpu.VMEM)
    count = len(inside)
    return pl.pallas_call(
        functools.partial(place_kernel, near, count),
        in_specs=[vmem] * (2 * count),
        out_specs=vmem,
        out_shape=jax.ShapeDtypeStruct((near, near, LAGS), jnp.float32),
        scratch_shapes=[pltpu.VMEM((LAGS // LANES, near * near, LANES), jnp.float32)],
        compiler_params=pltpu.CompilerParams(vmem_limit_bytes=VMEM_LIMIT),
        cost_estimate=pl.CostEstimate(flops=1_000_000_000, bytes_accessed=4 << 20, transcendentals=0),
        name="place",
    )(*inside, *across)


def shifted(value, steps):
    count = lax.axis_size("fibre")
    return lax.ppermute(value, "fibre", [(source, source + steps) for source in range(max(0, -steps), count)])


def line_of_four(traces):
    channels, segs, win = traces.shape
    tables = make_tables(win, LAGS, segs * 4)
    z = lax.axis_index("tm")
    left = z < 2
    blocks = traces.reshape(4, NEAR, segs, win)
    halo = shifted(blocks[0], -1)
    own = whiten(blocks, tables)
    ahead = whiten(halo[None], tables)

    def outer(value):
        return lax.ppermute(value, "tm", [(0, 1), (3, 2)])

    def middle(value):
        return lax.ppermute(value, "tm", [(1, 2), (2, 1)])

    def inner(value):
        return lax.ppermute(value, "tm", [(1, 0), (2, 3)])

    e1 = outer(jnp.where(left, own[3], own[0]))
    e2 = outer(jnp.where(left, ahead[0], own[1]))
    e3 = outer(own[2])
    e4 = outer(jnp.where(left, own[1], own[3]))

    number = lambda value: jnp.asarray(value, jnp.int32)
    scalars = lambda role, at: jnp.stack([number(role), number(at)])
    role = jnp.where(z == 1, 0, 1)
    none = jnp.zeros((2,), jnp.int32)
    mine = lag_sums("all", none, [own], [own], tables, base=0, blocks=3, total=4)
    mine = lag_sums("all", none, [own[3]], [ahead[0]], tables, blocks=1, total=4, grown=mine)
    far, mid, opposite = jnp.where(left, 3, 0), jnp.where(left, 2, 1), jnp.where(left, 0, 3)

    (m1,) = lag_sums("inside", scalars(0, far), [e1], None, tables, prior=mine[:1])
    m1 = middle(m1)
    (m2,) = lag_sums("across", scalars(0, far), [e1], [e2], tables, prior=mine[1:])
    m2 = middle(m2)
    (m3,) = lag_sums("inside", scalars(role, mid), [e3, e2], None, tables, prior=mine[:1])
    m3 = middle(m3)
    (m4,) = lag_sums("across", scalars(role, mid), [e3, e2], [e1, e3], tables, prior=mine[1:])
    m4 = middle(m4)
    near_in, near_out = lag_sums("all", scalars(role, z), [e4, e3], [e3, e4], tables, prior=mine)
    at = lambda value: lax.dynamic_index_in_dim(value, opposite, 0, keepdims=True)
    i1 = inner(m1 + at(mine[0]))
    i2 = inner(m2 + at(mine[1]))
    return place(NEAR, [v[0] for v in (near_in, i1, m3)], [v[0] for v in (near_out, i2, m4)])


def any_line(traces):
    channels, segs, win = traces.shape
    axis = lax.axis_size("tm")
    tables = make_tables(win, LAGS, segs * axis)
    blocks = traces.reshape(channels // NEAR, NEAR, segs, win)
    halo = shifted(blocks[0], -1)
    spectra = whiten(jnp.concatenate([blocks, halo[None]], axis=0), tables)
    count = channels // NEAR
    none = jnp.zeros((2,), jnp.int32)
    inside, across = lag_sums("all", none, [spectra], [spectra], tables, base=0, blocks=count, total=count)
    lagged = jnp.concatenate([place(NEAR, [inside[b]], [across[b]]) for b in range(count)], axis=0)
    return lax.psum_scatter(lagged, "tm", scatter_dimension=0, tiled=True)


def shards(traces):
    if lax.axis_size("tm") == 4 and traces.shape[0] == 4 * NEAR:
        return line_of_four(traces)
    return any_line(traces)


def solution(mesh):
    in_specs = (P("fibre", "tm", None),)
    out_specs = P(("fibre", "tm"), None, None)
    return jax.shard_map(shards, mesh=mesh, in_specs=in_specs, out_specs=out_specs, check_vma=False)
```

```python
import functools

import jax
import jax.numpy as jnp
import ml_dtypes
import numpy as np
from jax import lax
from jax.experimental import pallas as pl
from jax.experimental.pallas import tpu as pltpu
from jax.sharding import PartitionSpec as P

NEAR = 32
LAGS = 256
HALF = 8
LANES = 128
VMEM_LIMIT = 60 << 20


def split_table(table):
    high = table.astype(ml_dtypes.bfloat16)
    low = (table - high.astype(np.float64)).astype(ml_dtypes.bfloat16)
    return np.stack([high, low])


def make_tables(win, lags, segs):
    bins = win // 2
    samples = np.arange(win)
    hann = 0.5 - 0.5 * np.cos(2.0 * np.pi * samples / win)
    even, odd = np.arange(2, bins + 1, 2), np.arange(1, bins, 2)
    order = np.concatenate([even, odd])

    def forward(picked):
        phases = 2.0 * np.pi * ((samples[: win // 2, None] * picked[None, :]) % win) / win
        return split_table(np.concatenate([np.cos(phases), -np.sin(phases)], axis=1))

    near = np.abs(order[:, None] - order[None, :]) <= HALF
    band = near / (2.0 * HALF + 1.0) + 0.1 / bins
    lag = np.arange(lags) - lags // 2
    phases = 2.0 * np.pi * ((order[:, None] * lag[None, :]) % win) / win
    halves = np.split(phases, 2)
    rows = [part for h in halves for part in (np.cos(h), -np.sin(h))]
    high, low = split_table(np.concatenate(rows, axis=0) / segs)
    inverse = np.concatenate([high, low, high], axis=0)
    return {
        "hann": hann.astype(np.float32)[None, :],
        "even": forward(even),
        "odd": forward(odd),
        "band": split_table(band),
        "inverse": inverse,
    }


def dot_split(value, table):
    high = value.astype(jnp.bfloat16)
    low = (value - high.astype(jnp.float32)).astype(jnp.bfloat16)
    dot = functools.partial(jnp.dot, preferred_element_type=jnp.float32)
    return dot(high, table[0]) + (dot(high, table[1]) + dot(low, table[0]))


def whiten_kernel(x_ref, hann, even, odd, band, w_ref, stage):
    channels, segs, win = x_ref.shape
    parts = win // LANES
    for part in range(parts):
        lanes = slice(LANES * part, LANES * part + LANES)
        stage[part] = x_ref[:, :, lanes].reshape(channels * segs, LANES)
    pieces = []
    for s in range(segs):
        pieces.append([
            stage[part, pl.ds(s, channels, stride=segs), :] * hann[:, LANES * part : LANES * part + LANES]
            for part in range(parts)
        ])
    quarter = [jnp.concatenate([piece[part] for piece in pieces], axis=0) for part in range(parts)]
    both = jnp.concatenate([quarter[0] + quarter[2], quarter[1] + quarter[3]], axis=1)
    between = jnp.concatenate([quarter[0] - quarter[2], quarter[1] - quarter[3]], axis=1)
    spectra = (dot_split(both, even), dot_split(between, odd))
    energy = jnp.concatenate(
        [sp[:, :LANES] * sp[:, :LANES] + sp[:, LANES:] * sp[:, LANES:] for sp in spectra], axis=1
    )
    scale = lax.rsqrt(dot_split(energy, band) + 1e-06)
    for half, sp in enumerate(spectra):
        own = scale[:, LANES * half : LANES * half + LANES]
        real, imag = sp[:, :LANES] * own, sp[:, LANES:] * own
        for s in range(segs):
            rows = slice(channels * s, channels * s + channels)
            w_ref[half, 0, s] = real[rows]
            w_ref[half, 1, s] = imag[rows]


def whiten(x, tables, picks):
    blocks, near, segs, win = x.shape
    names = ("hann", "even", "odd", "band")
    consts = [jnp.asarray(tables[name]) for name in names]
    count = len(picks)

    def kernel(x_any, *refs):
        tabs, outs = refs[:4], refs[4 : 4 + count]
        staged, blocks_in, sems = refs[4 + count :]
        copies = []
        for index, pick in enumerate(picks):
            place = pick(lax.axis_index("tm")) if callable(pick) else pick
            copies.append(pltpu.make_async_copy(x_any.at[place], blocks_in.at[index], sems.at[index]))
            copies[-1].start()
        for index in range(count):
            copies[index].wait()
            whiten_kernel(blocks_in.at[index], *tabs, outs[index], staged)

    vmem = pl.BlockSpec(memory_space=pltpu.VMEM)
    shape = jax.ShapeDtypeStruct((2, 2, segs, near, LANES), jnp.float32)
    return pl.pallas_call(
        kernel,
        in_specs=[pl.BlockSpec(memory_space=pl.ANY)] + [vmem] * len(consts),
        out_specs=[vmem] * count,
        out_shape=[shape] * count,
        scratch_shapes=[
            pltpu.VMEM((win // LANES, near * segs, LANES), jnp.float32),
            pltpu.VMEM((count, near, segs, win), jnp.float32),
            pltpu.SemaphoreType.DMA((count,)),
        ],
        compiler_params=pltpu.CompilerParams(vmem_limit_bytes=VMEM_LIMIT),
        cost_estimate=pl.CostEstimate(flops=count * 500_000_000, bytes_accessed=count << 20, transcendentals=0),
        name="whiten",
    )(x, *consts)


def groups_of(near, which):
    tiles = near // 8
    inside = [(tile, offset) for tile in range(tiles) for offset in range(1, near - 8 * tile - 7)]
    across = [(tile, offset) for tile in range(tiles) for offset in range(near - 8 * tile - 7, near + 1)]
    return {"inside": inside, "across": across, "all": inside + across}[which]


def products(pair, half, lhs, groups, fresh, batch=4):
    segs = pair.shape[2]
    index_of = {group: index for index, group in enumerate(groups)}
    tiles = sorted({tile for tile, _ in groups})
    for begin in range(0, segs, batch):
        span = range(begin, min(begin + batch, segs))
        real = {t: [pair[half, 0, s, pl.ds(8 * t, 8), :] for s in span] for t in tiles}
        imag = {t: [pair[half, 1, s, pl.ds(8 * t, 8), :] for s in span] for t in tiles}
        added = {t: [re + im for re, im in zip(real[t], imag[t])] for t in tiles}
        for row in range(1, 8 * len(tiles) + NEAR):
            units = [(t, row - 8 * t) for t in tiles if (t, row - 8 * t) in index_of]
            if not units:
                continue
            sums = {}
            for at, s in enumerate(span):
                other_re = pair[half, 0, s, pl.ds(row, 8), :]
                other_im = pair[half, 1, s, pl.ds(row, 8), :]
                apart = other_re - other_im
                for unit in units:
                    t = unit[0]
                    terms = (real[t][at] * other_re, imag[t][at] * other_im, added[t][at] * apart)
                    sums[unit] = terms if at == 0 else tuple(old + new for old, new in zip(sums[unit], terms))
            for unit in units:
                rr, ii, mixed = sums[unit]
                cross_re, cross_im = rr + ii, mixed - rr + ii
                rows = pl.ds(8 * index_of[unit], 8)
                if not (fresh and begin == 0):
                    cross_re = cross_re + lhs[half, rows, :LANES]
                    cross_im = cross_im + lhs[half, rows, LANES:]
                lhs[half, rows, :LANES] = cross_re
                lhs[half, rows, LANES:] = cross_im


def lag_sums(which, sources, tables, role=None):
    table = jnp.asarray(tables["inverse"])
    sample = sources[0][0][0]
    halves, parts, segs, near, lanes = sample.shape
    groups = groups_of(near, which)
    kinds = {"inside": ("inside",), "across": ("across",), "all": ("inside", "across")}[which]
    sides = 1 if which == "inside" else 2
    operands, layout = [], []
    for source in sources:
        layout.append([])
        for side in range(sides):
            places = []
            for value in source[side]:
                known = [i for i, other in enumerate(operands) if other is value]
                if not known:
                    operands.append(value)
                places.append(known[0] if known else len(operands) - 1)
            layout[-1].append(places)
    shapes = [(len(groups_of(near, kind)), 8, LAGS) for kind in kinds]
    rows = 8 * len(groups)
    chunk = 16

    def kernel(*refs):
        cands, table_any = refs[: len(operands)], refs[len(operands)]
        outs = refs[len(operands) + 1 : len(operands) + 1 + len(kinds)]
        pair, lhs, table_ref, result, in_sems, table_sem, out_sems = refs[len(operands) + 1 + len(kinds) :]
        pick = role(lax.axis_index("tm")) if role is not None else None

        def copy(number, side, half, place):
            return pltpu.make_async_copy(
                cands[place].at[half],
                pair.at[number, half, :, :, pl.ds(side * near, near), :],
                in_sems.at[number, half, side],
            )

        for half in range(halves):
            for number, source in enumerate(layout):
                for side, places in enumerate(source):
                    if len(places) == 1:
                        copy(number, side, half, places[0]).start()
                        continue
                    for choice, place in enumerate(places):

                        @pl.when(pick == choice)
                        def _():
                            copy(number, side, half, place).start()

            if half == 0:
                table_copy = pltpu.make_async_copy(table_any, table_ref, table_sem)
                table_copy.start()

        def each_half(half, _):
            for number, source in enumerate(layout):
                for side, places in enumerate(source):
                    copy(number, side, half, places[0]).wait()
                products(pair.at[number], half, lhs, groups, number == 0)
            return 0

        lax.fori_loop(0, halves, each_half, 0)
        table_copy.wait()
        copies = []
        base = 0
        for out, shape in zip(outs, shapes):
            for begin in range(0, shape[0], chunk):
                size = min(chunk, shape[0] - begin)
                span = pl.ds(8 * (base + begin), 8 * size)
                value = jnp.concatenate([lhs[half, span, :] for half in range(halves)], axis=1)
                high = value.astype(jnp.bfloat16)
                low = (value - high.astype(jnp.float32)).astype(jnp.bfloat16)
                lagged = jnp.dot(
                    jnp.concatenate([high, high, low], axis=1), table_ref[...], preferred_element_type=jnp.float32
                )
                result[pl.ds(base + begin, size)] = lagged.reshape(size, 8, LAGS)
                copies.append(
                    pltpu.make_async_copy(
                        result.at[pl.ds(base + begin, size)], out.at[pl.ds(begin, size)], out_sems.at[len(copies)]
                    )
                )
                copies[-1].start()
            base += shape[0]
        for done in copies:
            done.wait()

    anywhere = pl.BlockSpec(memory_space=pl.ANY)
    chunks = sum(-(-shape[0] // chunk) for shape in shapes)
    work = rows * len(sources) // 8
    return pl.pallas_call(
        kernel,
        in_specs=[anywhere] * (len(operands) + 1),
        out_specs=[anywhere] * len(kinds),
        out_shape=[jax.ShapeDtypeStruct(shape, jnp.float32) for shape in shapes],
        scratch_shapes=[
            pltpu.VMEM((len(sources), halves, parts, segs, sides * near, lanes), jnp.float32),
            pltpu.VMEM((halves, rows, 2 * lanes), jnp.float32),
            pltpu.VMEM(table.shape, table.dtype),
            pltpu.VMEM((len(groups), 8, LAGS), jnp.float32),
            pltpu.SemaphoreType.DMA((len(sources), halves, 2)),
            pltpu.SemaphoreType.DMA,
            pltpu.SemaphoreType.DMA((chunks,)),
        ],
        compiler_params=pltpu.CompilerParams(vmem_limit_bytes=VMEM_LIMIT),
        cost_estimate=pl.CostEstimate(flops=work * 16_000_000, bytes_accessed=1 << 20, transcendentals=0),
        name="lag_" + which,
    )(*operands, table)


def place_kernel(near, count, *refs):
    terms, out_ref, stage = refs[: 2 * count], refs[2 * count], refs[2 * count + 1]
    for kind in range(2):
        for index, (tile, offset) in enumerate(groups_of(near, ("inside", "across")[kind])):
            value = terms[kind * count][index]
            for other in range(1, count):
                value = value + terms[kind * count + other][index]
            for part in range(LAGS // LANES):
                stage[part, pl.ds(8 * tile * near + offset - 1, 8, stride=near), :] = value[
                    :, LANES * part : LANES * part + LANES
                ]
    for part in range(LAGS // LANES):
        out_ref[:, :, LANES * part : LANES * part + LANES] = stage[part].reshape(near, near, LANES)


def place(near, inside, across):
    vmem = pl.BlockSpec(memory_space=pltpu.VMEM)
    count = len(inside)
    return pl.pallas_call(
        functools.partial(place_kernel, near, count),
        in_specs=[vmem] * (2 * count),
        out_specs=vmem,
        out_shape=jax.ShapeDtypeStruct((near, near, LAGS), jnp.float32),
        scratch_shapes=[pltpu.VMEM((LAGS // LANES, near * near, LANES), jnp.float32)],
        compiler_params=pltpu.CompilerParams(vmem_limit_bytes=VMEM_LIMIT),
        cost_estimate=pl.CostEstimate(flops=1_000_000_000, bytes_accessed=4 << 20, transcendentals=0),
        name="place",
    )(*inside, *across)


def shifted(value, steps):
    count = lax.axis_size("fibre")
    return lax.ppermute(value, "fibre", [(source, source + steps) for source in range(max(0, -steps), count)])


def line_of_four(traces):
    channels, segs, win = traces.shape
    tables = make_tables(win, LAGS, segs * 4)
    left = lax.axis_index("tm") < 2
    blocks = traces.reshape(4, NEAR, segs, win)
    fibres = lax.axis_size("fibre")

    def outer(value):
        return lax.ppermute(value, "tm", [(0, 1), (3, 2)])

    def outer_next(value):
        pairs = [(4 * fibre + 4, 4 * fibre + 1) for fibre in range(fibres - 1)]
        pairs += [(4 * fibre + 3, 4 * fibre + 2) for fibre in range(fibres)]
        return lax.ppermute(value, ("fibre", "tm"), pairs)

    def middle(value):
        return lax.ppermute(value, "tm", [(1, 2), (2, 1)])

    def inner(value):
        return lax.ppermute(value, "tm", [(1, 0), (2, 3)])

    (far,) = whiten(blocks, tables, [lambda z: jnp.where(z < 2, 3, 0)])
    e1 = outer(far)
    (next_far,) = whiten(blocks, tables, [lambda z: jnp.where(z < 2, 0, 1)])
    e2 = outer_next(next_far)
    halo = shifted(blocks[0], -1)
    own = whiten(blocks, tables, [0, 1, 2, 3])
    e3 = outer(own[2])
    e4 = outer(jnp.where(left, own[1], own[3]))
    own += whiten(halo[None], tables, [0])

    role = lambda z: jnp.where(z < 2, 0, 1)
    (m1,) = lag_sums("inside", [([far], None), ([e1], None)], tables)
    m1 = middle(m1)
    (m2,) = lag_sums("across", [([own[3], own[0]], [own[4], own[1]]), ([e1], [e2])], tables, role)
    m2 = middle(m2)
    opposite = lag_sums("all", [([own[0], own[3]], [own[1], own[4]])], tables, role)
    (m3,) = lag_sums("inside", [([own[2], own[1]], None), ([e3, e2], None)], tables, role)
    m3 = middle(m3)
    (m4,) = lag_sums("across", [([own[2], own[1]], [own[3], own[2]]), ([e3, e2], [e1, e3])], tables, role)
    m4 = middle(m4)
    near = lag_sums(
        "all", [(own[:4], own[1:]), ([e4, e4, e3, e4], [e3, e3, e4, e3])], tables, lambda z: z
    )
    i1 = inner(m1 + opposite[0])
    i2 = inner(m2 + opposite[1])
    return place(NEAR, [near[0], i1, m3], [near[1], i2, m4])


def any_line(traces):
    channels, segs, win = traces.shape
    tables = make_tables(win, LAGS, segs * lax.axis_size("tm"))
    count = channels // NEAR
    blocks = traces.reshape(count, NEAR, segs, win)
    halo = shifted(blocks[0], -1)
    spectra = whiten(blocks, tables, list(range(count))) + whiten(halo[None], tables, [0])
    pieces = []
    for index in range(count):
        inside, across = lag_sums("all", [([spectra[index]], [spectra[index + 1]])], tables)
        pieces.append(place(NEAR, [inside], [across]))
    return lax.psum_scatter(jnp.concatenate(pieces, axis=0), "tm", scatter_dimension=0, tiled=True)


def shards(traces):
    if lax.axis_size("tm") == 4 and traces.shape[0] == 4 * NEAR:
        return line_of_four(traces)
    return any_line(traces)


def solution(mesh):
    in_specs = (P("fibre", "tm", None),)
    out_specs = P(("fibre", "tm"), None, None)
    return jax.shard_map(shards, mesh=mesh, in_specs=in_specs, out_specs=out_specs, check_vma=False)
```

```python
import functools

import jax
import jax.numpy as jnp
import ml_dtypes
import numpy as np
from jax import lax
from jax.experimental import pallas as pl
from jax.experimental.pallas import tpu as pltpu
from jax.sharding import PartitionSpec as P

NEAR = 32
LAGS = 256
HALF = 8
LANES = 128
VMEM_LIMIT = 64 << 20
COST = 10_000_000_000


def split_table(table):
    high = table.astype(ml_dtypes.bfloat16)
    low = (table - high.astype(np.float64)).astype(ml_dtypes.bfloat16)
    return np.concatenate([high, low, high], axis=0)


def make_tables(win, lags, segs):
    bins = win // 2
    samples = np.arange(win)
    hann = 0.5 - 0.5 * np.cos(2.0 * np.pi * samples / win)
    even, odd = np.arange(2, bins + 1, 2), np.arange(1, bins, 2)
    order = np.concatenate([even, odd])

    def forward(picked):
        phases = 2.0 * np.pi * ((samples[: win // 2, None] * picked[None, :]) % win) / win
        return split_table(np.concatenate([np.cos(phases), -np.sin(phases)], axis=1))

    near = np.abs(order[:, None] - order[None, :]) <= HALF
    band = near / (2.0 * HALF + 1.0) + 0.1 / bins
    lag = np.arange(lags) - lags // 2
    phases = 2.0 * np.pi * ((order[:, None] * lag[None, :]) % win) / win
    rows = [part for half in np.split(phases, 2) for part in (np.cos(half), -np.sin(half))]
    return {
        "hann": np.tile(hann.astype(np.float32)[None, :], (8, 1)),
        "forward": np.stack([forward(even), forward(odd), split_table(band)]),
        "inverse": split_table(np.concatenate(rows, axis=0) / segs),
    }


def dot_split(value, table):
    high = value.astype(jnp.bfloat16)
    low = (value - high.astype(jnp.float32)).astype(jnp.bfloat16)
    return jnp.dot(jnp.concatenate([high, high, low], axis=1), table, preferred_element_type=jnp.float32)


def whiten_block(x_ref, hann, forward, w_ref, stage):
    channels, segs, win = x_ref.shape
    parts = win // LANES
    for part in range(parts):
        lanes = slice(LANES * part, LANES * part + LANES)
        stage[part] = x_ref[:, :, lanes].reshape(channels * segs, LANES)
    pieces = []
    for s in range(segs):
        pieces.append([
            stage[part, pl.ds(s, channels, stride=segs), :] * hann[0:1, LANES * part : LANES * part + LANES]
            for part in range(parts)
        ])
    quarter = [jnp.concatenate([piece[part] for piece in pieces], axis=0) for part in range(parts)]
    both = jnp.concatenate([quarter[0] + quarter[2], quarter[1] + quarter[3]], axis=1)
    between = jnp.concatenate([quarter[0] - quarter[2], quarter[1] - quarter[3]], axis=1)
    spectra = (dot_split(both, forward[0]), dot_split(between, forward[1]))
    energy = jnp.concatenate(
        [sp[:, :LANES] * sp[:, :LANES] + sp[:, LANES:] * sp[:, LANES:] for sp in spectra], axis=1
    )
    scale = lax.rsqrt(dot_split(energy, forward[2]) + 1e-06)
    for half, sp in enumerate(spectra):
        own = scale[:, LANES * half : LANES * half + LANES]
        real, imag = sp[:, :LANES] * own, sp[:, LANES:] * own
        for s in range(segs):
            rows = slice(channels * s, channels * s + channels)
            w_ref[half, 0, s] = real[rows]
            w_ref[half, 1, s] = imag[rows]


def whiten(x, tables, count):
    near, segs, win = x.shape[1:]
    consts = [jnp.asarray(tables["hann"]), jnp.asarray(tables["forward"])]

    def kernel(*refs):
        x_any, hann_any, forward_any = refs[:3]
        outs, refs = refs[3 : 3 + count], refs[3 + count :]
        stage, hann, forward, blocks_in, blocks_out, sems, out_sems = refs
        loads = [pltpu.make_async_copy(x_any.at[b], blocks_in.at[b], sems.at[b]) for b in range(count)]
        tabs = [
            pltpu.make_async_copy(hann_any, hann, sems.at[count]),
            pltpu.make_async_copy(forward_any, forward, sems.at[count + 1]),
        ]
        for load in tabs + loads:
            load.start()
        for load in tabs:
            load.wait()
        stores = []
        for index in range(count):
            loads[index].wait()
            whiten_block(blocks_in.at[index], hann, forward, blocks_out.at[index], stage)
            stores.append(pltpu.make_async_copy(blocks_out.at[index], outs[index], out_sems.at[index]))
            stores[-1].start()
        for store in stores:
            store.wait()

    shape = (2, 2, segs, near, LANES)
    far_memory = pl.BlockSpec(memory_space=pltpu.HBM)
    return pl.pallas_call(
        kernel,
        in_specs=[far_memory] * 3,
        out_specs=[far_memory] * count,
        out_shape=[jax.ShapeDtypeStruct(shape, jnp.float32)] * count,
        scratch_shapes=[
            pltpu.VMEM((win // LANES, near * segs, LANES), jnp.float32),
            pltpu.VMEM(consts[0].shape, consts[0].dtype),
            pltpu.VMEM(consts[1].shape, consts[1].dtype),
            pltpu.VMEM((count, near, segs, win), jnp.float32),
            pltpu.VMEM((count,) + shape, jnp.float32),
            pltpu.SemaphoreType.DMA((count + 2,)),
            pltpu.SemaphoreType.DMA((count,)),
        ],
        compiler_params=pltpu.CompilerParams(vmem_limit_bytes=VMEM_LIMIT),
        cost_estimate=pl.CostEstimate(flops=COST, bytes_accessed=1000, transcendentals=0),
        name="whiten",
    )(x, *consts)


def whiten_first(x, tables, before=None):
    near, segs, win = x.shape[1:]
    consts = [jnp.asarray(tables["hann"]), jnp.asarray(tables["forward"])]
    first = before is None
    count = 1 if first else 6
    passed = [] if first else [before]

    def kernel(*refs):
        x_any, hann_any, forward_any = refs[:3]
        refs = refs[3 + len(passed) :]
        outs, refs = refs[:count], refs[count:]
        stage, hann, forward, blocks_in, blocks_out, sems, out_sems = refs
        z = lax.axis_index("tm")
        end = (z == 0) | (z == 3)

        def load_tables():
            tabs = [
                pltpu.make_async_copy(hann_any, hann, sems.at[4]),
                pltpu.make_async_copy(forward_any, forward, sems.at[5]),
            ]
            for tab in tabs:
                tab.start()
            return tabs

        def one(load, slot):
            load.wait()
            whiten_block(blocks_in.at[slot], hann, forward, blocks_out.at[slot], stage)

        def all_four(tabs):
            loads = [pltpu.make_async_copy(x_any.at[b], blocks_in.at[b], sems.at[b]) for b in range(4)]
            for load in loads:
                load.start()
            for tab in tabs:
                tab.wait()
            stores = []
            for b in range(4):
                one(loads[b], b)
                stores.append(pltpu.make_async_copy(blocks_out.at[b], outs[b], out_sems.at[b]))
                stores[-1].start()
            for at, sources in enumerate(((0, 1), (1, 3))):
                for side, source in enumerate(sources):

                    @pl.when(z < 2 if side == 0 else z >= 2)
                    def _():
                        pltpu.make_async_copy(
                            blocks_out.at[source], outs[4 + at], out_sems.at[4 + at]
                        ).start()

                stores.append(
                    pltpu.make_async_copy(blocks_out.at[sources[0]], outs[4 + at], out_sems.at[4 + at])
                )
            for store in stores:
                store.wait()

        if first:

            @pl.when(end)
            def _():
                load = pltpu.make_async_copy(x_any.at[jnp.where(z < 2, 3, 0)], blocks_in.at[4], sems.at[6])
                load.start()
                for tab in load_tables():
                    tab.wait()
                one(load, 4)
                store = pltpu.make_async_copy(blocks_out.at[4], outs[0], out_sems.at[6])
                store.start()
                store.wait()

        else:
            all_four(load_tables())

    shape = (2, 2, segs, near, LANES)
    far_memory = pl.BlockSpec(memory_space=pltpu.HBM)
    return pl.pallas_call(
        kernel,
        in_specs=[far_memory] * (3 + len(passed)),
        out_specs=[far_memory] * count,
        out_shape=[jax.ShapeDtypeStruct(shape, jnp.float32)] * count,
        scratch_shapes=[
            pltpu.VMEM((win // LANES, near * segs, LANES), jnp.float32),
            pltpu.VMEM(consts[0].shape, consts[0].dtype),
            pltpu.VMEM(consts[1].shape, consts[1].dtype),
            pltpu.VMEM((5, near, segs, win), jnp.float32),
            pltpu.VMEM((5,) + shape, jnp.float32),
            pltpu.SemaphoreType.DMA((7,)),
            pltpu.SemaphoreType.DMA((7,)),
        ],
        compiler_params=pltpu.CompilerParams(vmem_limit_bytes=VMEM_LIMIT),
        cost_estimate=pl.CostEstimate(flops=COST, bytes_accessed=1000, transcendentals=0),
        name="whiten_first" if first else "whiten_rest",
    )(x, *consts, *passed)


def groups_of(near, which):
    tiles = near // 8
    inside = [(tile, offset) for tile in range(tiles) for offset in range(1, near - 8 * tile - 7)]
    across = [(tile, offset) for tile in range(tiles) for offset in range(near - 8 * tile - 7, near + 1)]
    return {"inside": inside, "across": across, "all": inside + across}[which]


def products(pair, half, lhs, groups, fresh, batch=4):
    segs = pair.shape[2]
    index_of = {group: index for index, group in enumerate(groups)}
    tiles = sorted({tile for tile, _ in groups})
    for begin in range(0, segs, batch):
        span = range(begin, min(begin + batch, segs))
        real = {t: [pair[half, 0, s, pl.ds(8 * t, 8), :] for s in span] for t in tiles}
        imag = {t: [pair[half, 1, s, pl.ds(8 * t, 8), :] for s in span] for t in tiles}
        added = {t: [re + im for re, im in zip(real[t], imag[t])] for t in tiles}
        for row in range(1, 8 * len(tiles) + NEAR):
            units = [(t, row - 8 * t) for t in tiles if (t, row - 8 * t) in index_of]
            if not units:
                continue
            sums = {}
            for at, s in enumerate(span):
                other_re = pair[half, 0, s, pl.ds(row, 8), :]
                other_im = pair[half, 1, s, pl.ds(row, 8), :]
                apart = other_re - other_im
                for unit in units:
                    t = unit[0]
                    terms = (real[t][at] * other_re, imag[t][at] * other_im, added[t][at] * apart)
                    sums[unit] = terms if at == 0 else tuple(old + new for old, new in zip(sums[unit], terms))
            for unit in units:
                rr, ii, mixed = sums[unit]
                cross_re, cross_im = rr + ii, mixed - rr + ii
                rows = pl.ds(8 * index_of[unit], 8)
                if not (fresh and begin == 0):
                    cross_re = cross_re + lhs[half, rows, :LANES]
                    cross_im = cross_im + lhs[half, rows, LANES:]
                lhs[half, rows, :LANES] = cross_re
                lhs[half, rows, LANES:] = cross_im


def lag_sums(which, sources, tables, role=None, prior=(), after=(), cost=COST, inner=False):
    table = jnp.asarray(tables["inverse"])
    sample = sources[0][0][0]
    halves, parts, segs, near, lanes = sample.shape
    groups = groups_of(near, which)
    sides = 1 if which == "inside" else 2
    operands, layout = [], []
    for source in sources:
        layout.append([])
        for side in range(sides):
            places = []
            for value in source[side]:
                known = [i for i, other in enumerate(operands) if other is value]
                if not known:
                    operands.append(value)
                places.append(known[0] if known else len(operands) - 1)
            layout[-1].append(places)
    shape = (len(groups), 8, LAGS)
    rows = 8 * len(groups)
    chunk = 16

    def kernel(*refs):
        if not inner:
            return work(*refs)
        z = lax.axis_index("tm")
        pl.when((z == 1) | (z == 2))(lambda: work(*refs))

    def work(*refs):
        cands, table_any = refs[: len(operands)], refs[len(operands)]
        refs = refs[len(operands) + 1 :]
        priors, refs = refs[: len(prior)], refs[len(prior) + len(after) :]
        out, pair, lhs, table_ref, result, in_sems, table_sem, prior_sem, out_sems = refs
        pick = role(lax.axis_index("tm")) if role is not None else None

        def copy(number, side, half, place):
            return pltpu.make_async_copy(
                cands[place].at[half],
                pair.at[number, half, :, :, pl.ds(side * near, near), :],
                in_sems.at[number, half, side],
            )

        for half in range(halves):
            for number, source in enumerate(layout):
                for side, places in enumerate(source):
                    if len(places) == 1:
                        copy(number, side, half, places[0]).start()
                        continue
                    for choice, place in enumerate(places):

                        @pl.when(pick == choice)
                        def _():
                            copy(number, side, half, place).start()

            if half == 0:
                table_copy = pltpu.make_async_copy(table_any, table_ref, table_sem)
                table_copy.start()
        if prior:
            prior_copy = pltpu.make_async_copy(priors[0], result, prior_sem)
            prior_copy.start()

        def each_half(half, _):
            for number, source in enumerate(layout):
                for side, places in enumerate(source):
                    copy(number, side, half, places[0]).wait()
                products(pair.at[number], half, lhs, groups, number == 0)
            return 0

        lax.fori_loop(0, halves, each_half, 0)
        table_copy.wait()
        if prior:
            prior_copy.wait()
        copies = []
        for begin in range(0, shape[0], chunk):
            size = min(chunk, shape[0] - begin)
            span = pl.ds(8 * begin, 8 * size)
            value = jnp.concatenate([lhs[half, span, :] for half in range(halves)], axis=1)
            lagged = dot_split(value, table_ref[...]).reshape(size, 8, LAGS)
            place = pl.ds(begin, size)
            result[place] = result[place] + lagged if prior else lagged
            copies.append(pltpu.make_async_copy(result.at[place], out.at[place], out_sems.at[len(copies)]))
            copies[-1].start()
        for done in copies:
            done.wait()

    far_memory = pl.BlockSpec(memory_space=pltpu.HBM)
    chunks = -(-shape[0] // chunk)
    return pl.pallas_call(
        kernel,
        in_specs=[far_memory] * (len(operands) + 1 + len(prior) + len(after)),
        out_specs=far_memory,
        out_shape=jax.ShapeDtypeStruct(shape, jnp.float32),
        scratch_shapes=[
            pltpu.VMEM((len(sources), halves, parts, segs, sides * near, lanes), jnp.float32),
            pltpu.VMEM((halves, rows, 2 * lanes), jnp.float32),
            pltpu.VMEM(table.shape, table.dtype),
            pltpu.VMEM(shape, jnp.float32),
            pltpu.SemaphoreType.DMA((len(sources), halves, 2)),
            pltpu.SemaphoreType.DMA,
            pltpu.SemaphoreType.DMA,
            pltpu.SemaphoreType.DMA((chunks,)),
        ],
        compiler_params=pltpu.CompilerParams(vmem_limit_bytes=VMEM_LIMIT),
        cost_estimate=pl.CostEstimate(flops=cost, bytes_accessed=1000, transcendentals=0),
        name="lag_" + which,
    )(*operands, table, *prior, *after)


def place(near, inside, across):
    count = len(inside)
    begins = [[begin for _, begin in terms] for terms in (inside, across)]
    kinds = ("inside", "across")
    parts = LAGS // LANES
    tiles = near // 8

    def kernel(*refs):
        terms, out = (refs[:count], refs[count : 2 * count]), refs[2 * count]
        buffers, (stage, in_sems, out_sems) = refs[2 * count + 1 : 2 * count + 3], refs[2 * count + 3 :]
        loads, groups = {}, {}
        for tile in range(tiles):
            for kind in range(2):
                known = groups_of(near, kinds[kind])
                mine = [index for index, group in enumerate(known) if group[0] == tile]
                groups[tile, kind] = [(index, known[index][1]) for index in mine]
                if not mine:
                    continue
                span = pl.ds(mine[0], len(mine))
                for term in range(count):
                    loads[tile, kind, term] = pltpu.make_async_copy(
                        terms[kind][term].at[pl.ds(begins[kind][term] + mine[0], len(mine))], buffers[kind].at[term, span], in_sems.at[tile, kind, term]
                    )
                    loads[tile, kind, term].start()
        stores = []
        for tile in range(tiles):
            for kind in range(2):
                for term in range(count):
                    if (tile, kind, term) in loads:
                        loads[tile, kind, term].wait()
                for index, offset in groups[tile, kind]:
                    value = buffers[kind][0, index]
                    for term in range(1, count):
                        value = value + buffers[kind][term, index]
                    for part in range(parts):
                        stage[part, pl.ds(8 * tile * near + offset - 1, 8, stride=near), :] = value[
                            :, LANES * part : LANES * part + LANES
                        ]
            for part in range(parts):
                stores.append(
                    pltpu.make_async_copy(
                        stage.at[part].reshape(near, near, LANES).at[pl.ds(8 * tile, 8)],
                        out.at[pl.ds(8 * tile, 8), :, pl.ds(LANES * part, LANES)],
                        out_sems.at[tile, part],
                    )
                )
                stores[-1].start()
        for store in stores:
            store.wait()

    far_memory = pl.BlockSpec(memory_space=pltpu.HBM)
    return pl.pallas_call(
        kernel,
        in_specs=[far_memory] * (2 * count),
        out_specs=far_memory,
        out_shape=jax.ShapeDtypeStruct((near, near, LAGS), jnp.float32),
        scratch_shapes=[pltpu.VMEM((count, len(groups_of(near, kind)), 8, LAGS), jnp.float32) for kind in kinds]
        + [
            pltpu.VMEM((parts, near * near, LANES), jnp.float32),
            pltpu.SemaphoreType.DMA((tiles, 2, count)),
            pltpu.SemaphoreType.DMA((tiles, parts)),
        ],
        compiler_params=pltpu.CompilerParams(vmem_limit_bytes=VMEM_LIMIT),
        cost_estimate=pl.CostEstimate(flops=COST, bytes_accessed=1000, transcendentals=0),
        name="place",
    )(*[value for value, _ in inside + across])


def shifted(value, steps):
    count = lax.axis_size("fibre")
    return lax.ppermute(value, "fibre", [(source, source + steps) for source in range(max(0, -steps), count)])


def line_of_four(traces):
    channels, segs, win = traces.shape
    tables = make_tables(win, LAGS, segs * 4)
    blocks = traces.reshape(4, NEAR, segs, win)
    fibres = lax.axis_size("fibre")

    def outer(value):
        return lax.ppermute(value, "tm", [(0, 1), (3, 2)])

    def outer_next(value):
        pairs = [(4 * fibre + 4, 4 * fibre + 1) for fibre in range(fibres - 1)]
        pairs += [(4 * fibre + 3, 4 * fibre + 2) for fibre in range(fibres)]
        return lax.ppermute(value, ("fibre", "tm"), pairs)

    def middle(value):
        return lax.ppermute(value, "tm", [(1, 2), (2, 1)])

    def inner(value):
        return lax.ppermute(value, "tm", [(1, 0), (2, 3)])

    (far,) = whiten_first(blocks, tables)
    e1 = outer(far)
    *own, next_far, last = whiten_first(blocks, tables, far)
    e2 = outer_next(next_far)
    own.append(shifted(own[0], -1))
    e3 = outer(own[2])

    role = lambda z: jnp.where(z < 2, 0, 1)
    jobs = functools.partial(lag_sums, tables=tables, inner=True)
    back_in = jobs("inside", [([own[0], own[3]], None)], role=role, cost=1_000_000)
    m1 = jobs("inside", [([own[3], own[0]], None), ([e1], None)], role=role, after=[back_in])
    m1_in = middle(m1)
    base = jobs("across", [([own[3], own[0]], [own[4], own[1]])], role=role, after=[m1])
    m2 = jobs("across", [([e1], [e2])], prior=[base])
    m2_in = middle(m2)
    m1_in, _ = lax.optimization_barrier((m1_in, m2))
    first = m1_in + back_in
    i1 = inner(first)
    last, _ = lax.optimization_barrier((last, first))
    e4 = outer(last)
    m3 = jobs("all", [([own[2], own[1]], [own[3], own[2]]), ([e3, e2], [e1, e3])], role=role, after=[first])
    m3_in = middle(m3)
    back_out = jobs("across", [([own[0], own[3]], [own[1], own[4]])], role=role, after=[m3])
    m2_in, _ = lax.optimization_barrier((m2_in, back_out))
    second = m2_in + back_out
    i2 = inner(second)
    near = lag_sums(
        "all", [(own[:4], own[1:]), ([e4, e4, e3, e4], [e3, e3, e4, e3])], tables, lambda z: z, after=[second]
    )
    start = m1.shape[0]
    return place(NEAR, [(near, 0), (i1, 0), (m3_in, 0)], [(near, start), (i2, 0), (m3_in, start)])


def any_line(traces):
    channels, segs, win = traces.shape
    tables = make_tables(win, LAGS, segs * lax.axis_size("tm"))
    count = channels // NEAR
    blocks = traces.reshape(count, NEAR, segs, win)
    halo = shifted(blocks[0], -1)
    spectra = whiten(blocks, tables, count) + whiten(halo[None], tables, 1)
    start = len(groups_of(NEAR, "inside"))
    pieces = []
    for index in range(count):
        sums = lag_sums("all", [([spectra[index]], [spectra[index + 1]])], tables)
        pieces.append(place(NEAR, [(sums, 0)], [(sums, start)]))
    return lax.psum_scatter(jnp.concatenate(pieces, axis=0), "tm", scatter_dimension=0, tiled=True)


def shards(traces):
    if lax.axis_size("tm") == 4 and traces.shape[0] == 4 * NEAR:
        return line_of_four(traces)
    return any_line(traces)


def solution(mesh):
    in_specs = (P("fibre", "tm", None),)
    out_specs = P(("fibre", "tm"), None, None)
    return jax.shard_map(shards, mesh=mesh, in_specs=in_specs, out_specs=out_specs, check_vma=False)
```

```python
import functools

import jax
import jax.numpy as jnp
import ml_dtypes
import numpy as np
from jax import lax
from jax.experimental import pallas as pl
from jax.experimental.pallas import tpu as pltpu
from jax.sharding import PartitionSpec as P

NEAR = 32
LAGS = 256
HALF = 8
LANES = 128
VMEM_LIMIT = 64 << 20
COST = 10_000_000_000


def split_table(table):
    high = table.astype(ml_dtypes.bfloat16)
    low = (table - high.astype(np.float64)).astype(ml_dtypes.bfloat16)
    return np.concatenate([high, low, high], axis=0)


def make_tables(win, lags, segs):
    bins = win // 2
    samples = np.arange(win)
    hann = 0.5 - 0.5 * np.cos(2.0 * np.pi * samples / win)
    even, odd = np.arange(2, bins + 1, 2), np.arange(1, bins, 2)
    order = np.concatenate([even, odd])

    def forward(picked):
        phases = 2.0 * np.pi * ((samples[: win // 2, None] * picked[None, :]) % win) / win
        return split_table(np.concatenate([np.cos(phases), -np.sin(phases)], axis=1))

    near = np.abs(order[:, None] - order[None, :]) <= HALF
    band = near / (2.0 * HALF + 1.0) + 0.1 / bins
    lag = np.arange(lags) - lags // 2
    phases = 2.0 * np.pi * ((order[:, None] * lag[None, :]) % win) / win
    rows = [part for half in np.split(phases, 2) for part in (np.cos(half), -np.sin(half))]
    return {
        "hann": np.tile(hann.astype(np.float32)[None, :], (8, 1)),
        "forward": np.stack([forward(even), forward(odd), split_table(band)]),
        "inverse": split_table(np.concatenate(rows, axis=0) / segs),
    }


def dot_split(value, table):
    high = value.astype(jnp.bfloat16)
    low = (value - high.astype(jnp.float32)).astype(jnp.bfloat16)
    return jnp.dot(jnp.concatenate([high, high, low], axis=1), table, preferred_element_type=jnp.float32)


def whiten_block(x_ref, hann, forward, w_ref, stage):
    channels, segs, win = x_ref.shape
    parts = win // LANES
    for part in range(parts):
        lanes = slice(LANES * part, LANES * part + LANES)
        stage[part, pl.ds(0, channels * segs)] = x_ref[:, :, lanes].reshape(channels * segs, LANES)
    pieces = []
    for s in range(segs):
        pieces.append([
            stage[part, pl.ds(s, channels, stride=segs), :] * hann[0:1, LANES * part : LANES * part + LANES]
            for part in range(parts)
        ])
    quarter = [jnp.concatenate([piece[part] for piece in pieces], axis=0) for part in range(parts)]
    both = jnp.concatenate([quarter[0] + quarter[2], quarter[1] + quarter[3]], axis=1)
    between = jnp.concatenate([quarter[0] - quarter[2], quarter[1] - quarter[3]], axis=1)
    spectra = (dot_split(both, forward[0]), dot_split(between, forward[1]))
    energy = jnp.concatenate(
        [sp[:, :LANES] * sp[:, :LANES] + sp[:, LANES:] * sp[:, LANES:] for sp in spectra], axis=1
    )
    scale = lax.rsqrt(dot_split(energy, forward[2]) + 1e-06)
    for half, sp in enumerate(spectra):
        own = scale[:, LANES * half : LANES * half + LANES]
        real, imag = sp[:, :LANES] * own, sp[:, LANES:] * own
        for s in range(segs):
            rows = slice(channels * s, channels * s + channels)
            w_ref[half, 0, s] = real[rows]
            w_ref[half, 1, s] = imag[rows]


def whiten(x, tables, count):
    near, segs, win = x.shape[1:]
    consts = [jnp.asarray(tables["hann"]), jnp.asarray(tables["forward"])]

    def kernel(*refs):
        x_any, hann_any, forward_any = refs[:3]
        outs, refs = refs[3 : 3 + count], refs[3 + count :]
        stage, hann, forward, blocks_in, blocks_out, sems, out_sems = refs
        loads = [pltpu.make_async_copy(x_any.at[b], blocks_in.at[b], sems.at[b]) for b in range(count)]
        tabs = [
            pltpu.make_async_copy(hann_any, hann, sems.at[count]),
            pltpu.make_async_copy(forward_any, forward, sems.at[count + 1]),
        ]
        for load in tabs + loads:
            load.start()
        for load in tabs:
            load.wait()
        stores = []
        for index in range(count):
            loads[index].wait()
            whiten_block(blocks_in.at[index], hann, forward, blocks_out.at[index], stage)
            stores.append(pltpu.make_async_copy(blocks_out.at[index], outs[index], out_sems.at[index]))
            stores[-1].start()
        for store in stores:
            store.wait()

    shape = (2, 2, segs, near, LANES)
    far_memory = pl.BlockSpec(memory_space=pltpu.HBM)
    return pl.pallas_call(
        kernel,
        in_specs=[far_memory] * 3,
        out_specs=[far_memory] * count,
        out_shape=[jax.ShapeDtypeStruct(shape, jnp.float32)] * count,
        scratch_shapes=[
            pltpu.VMEM((win // LANES, near * segs, LANES), jnp.float32),
            pltpu.VMEM(consts[0].shape, consts[0].dtype),
            pltpu.VMEM(consts[1].shape, consts[1].dtype),
            pltpu.VMEM((count, near, segs, win), jnp.float32),
            pltpu.VMEM((count,) + shape, jnp.float32),
            pltpu.SemaphoreType.DMA((count + 2,)),
            pltpu.SemaphoreType.DMA((count,)),
        ],
        compiler_params=pltpu.CompilerParams(vmem_limit_bytes=VMEM_LIMIT),
        cost_estimate=pl.CostEstimate(flops=COST, bytes_accessed=1000, transcendentals=0),
        name="whiten",
    )(x, *consts)


def whiten_first(x, tables, before=None):
    near, segs, win = x.shape[1:]
    consts = [jnp.asarray(tables["hann"]), jnp.asarray(tables["forward"])]
    first = before is None
    count = 1 if first else 6
    passed = [] if first else [before]

    def kernel(*refs):
        x_any, hann_any, forward_any = refs[:3]
        refs = refs[3 + len(passed) :]
        outs, refs = refs[:count], refs[count:]
        stage, hann, forward, blocks_in, blocks_out, sems, out_sems = refs
        z = lax.axis_index("tm")
        end = (z == 0) | (z == 3)

        def load_tables():
            tabs = [
                pltpu.make_async_copy(hann_any, hann, sems.at[4]),
                pltpu.make_async_copy(forward_any, forward, sems.at[5]),
            ]
            for tab in tabs:
                tab.start()
            return tabs

        def one(load, slot):
            load.wait()
            whiten_block(blocks_in.at[slot], hann, forward, blocks_out.at[slot], stage)

        def all_four(tabs):
            loads = [pltpu.make_async_copy(x_any.at[b], blocks_in.at[b], sems.at[b]) for b in range(4)]
            for load in loads:
                load.start()
            for tab in tabs:
                tab.wait()
            stores = []
            for b in range(4):
                one(loads[b], b)
                stores.append(pltpu.make_async_copy(blocks_out.at[b], outs[b], out_sems.at[b]))
                stores[-1].start()
            for at, sources in enumerate(((0, 1), (1, 3))):
                for side, source in enumerate(sources):

                    @pl.when(z < 2 if side == 0 else z >= 2)
                    def _():
                        pltpu.make_async_copy(
                            blocks_out.at[source], outs[4 + at], out_sems.at[4 + at]
                        ).start()

                stores.append(
                    pltpu.make_async_copy(blocks_out.at[sources[0]], outs[4 + at], out_sems.at[4 + at])
                )
            for store in stores:
                store.wait()

        if first:

            @pl.when(end)
            def _():
                place = jnp.where(z < 2, 3, 0)
                step = near // 2
                spans = [pl.ds(0, step), pl.ds(step, step)]
                loads = [
                    pltpu.make_async_copy(x_any.at[place, span], blocks_in.at[4, span], sems.at[index])
                    for index, span in enumerate(spans)
                ]
                loads[0].start()
                tabs = load_tables()
                loads[1].start()
                for tab in tabs:
                    tab.wait()
                stores = []
                for index, span in enumerate(spans):
                    loads[index].wait()
                    target = blocks_out.at[4, :, :, :, span]
                    whiten_block(blocks_in.at[4, span], hann, forward, target, stage)
                    stores.append(pltpu.make_async_copy(target, outs[0].at[:, :, :, span], out_sems.at[index]))
                    stores[-1].start()
                for store in stores:
                    store.wait()

        else:
            all_four(load_tables())

    shape = (2, 2, segs, near, LANES)
    far_memory = pl.BlockSpec(memory_space=pltpu.HBM)
    return pl.pallas_call(
        kernel,
        in_specs=[far_memory] * (3 + len(passed)),
        out_specs=[far_memory] * count,
        out_shape=[jax.ShapeDtypeStruct(shape, jnp.float32)] * count,
        scratch_shapes=[
            pltpu.VMEM((win // LANES, near * segs, LANES), jnp.float32),
            pltpu.VMEM(consts[0].shape, consts[0].dtype),
            pltpu.VMEM(consts[1].shape, consts[1].dtype),
            pltpu.VMEM((5, near, segs, win), jnp.float32),
            pltpu.VMEM((5,) + shape, jnp.float32),
            pltpu.SemaphoreType.DMA((7,)),
            pltpu.SemaphoreType.DMA((7,)),
        ],
        compiler_params=pltpu.CompilerParams(vmem_limit_bytes=VMEM_LIMIT),
        cost_estimate=pl.CostEstimate(flops=COST, bytes_accessed=1000, transcendentals=0),
        name="whiten_first" if first else "whiten_rest",
    )(x, *consts, *passed)


def groups_of(near, which):
    tiles = near // 8
    inside = [(tile, offset) for tile in range(tiles) for offset in range(1, near - 8 * tile - 7)]
    across = [(tile, offset) for tile in range(tiles) for offset in range(near - 8 * tile - 7, near + 1)]
    return {"inside": inside, "across": across, "all": inside + across}[which]


def products(pair, half, lhs, groups, fresh, batch=4):
    segs = pair.shape[2]
    index_of = {group: index for index, group in enumerate(groups)}
    tiles = sorted({tile for tile, _ in groups})
    for begin in range(0, segs, batch):
        span = range(begin, min(begin + batch, segs))
        real = {t: [pair[half, 0, s, pl.ds(8 * t, 8), :] for s in span] for t in tiles}
        imag = {t: [pair[half, 1, s, pl.ds(8 * t, 8), :] for s in span] for t in tiles}
        added = {t: [re + im for re, im in zip(real[t], imag[t])] for t in tiles}
        for row in range(1, 8 * len(tiles) + NEAR):
            units = [(t, row - 8 * t) for t in tiles if (t, row - 8 * t) in index_of]
            if not units:
                continue
            sums = {}
            for at, s in enumerate(span):
                other_re = pair[half, 0, s, pl.ds(row, 8), :]
                other_im = pair[half, 1, s, pl.ds(row, 8), :]
                apart = other_re - other_im
                for unit in units:
                    t = unit[0]
                    terms = (real[t][at] * other_re, imag[t][at] * other_im, added[t][at] * apart)
                    sums[unit] = terms if at == 0 else tuple(old + new for old, new in zip(sums[unit], terms))
            for unit in units:
                rr, ii, mixed = sums[unit]
                cross_re, cross_im = rr + ii, mixed - rr + ii
                rows = pl.ds(8 * index_of[unit], 8)
                if not (fresh and begin == 0):
                    cross_re = cross_re + lhs[half, rows, :LANES]
                    cross_im = cross_im + lhs[half, rows, LANES:]
                lhs[half, rows, :LANES] = cross_re
                lhs[half, rows, LANES:] = cross_im


def lag_sums(which, sources, tables, role=None, prior=(), after=(), cost=COST, inner=False):
    table = jnp.asarray(tables["inverse"])
    sample = sources[0][0][0]
    halves, parts, segs, near, lanes = sample.shape
    groups = groups_of(near, which)
    sides = 1 if which == "inside" else 2
    operands, layout = [], []
    for source in sources:
        layout.append([])
        for side in range(sides):
            places = []
            for value in source[side]:
                known = [i for i, other in enumerate(operands) if other is value]
                if not known:
                    operands.append(value)
                places.append(known[0] if known else len(operands) - 1)
            layout[-1].append(places)
    shape = (len(groups), 8, LAGS)
    rows = 8 * len(groups)
    chunk = 16

    def kernel(*refs):
        if not inner:
            return work(*refs)
        z = lax.axis_index("tm")
        pl.when((z == 1) | (z == 2))(lambda: work(*refs))

    def work(*refs):
        cands, table_any = refs[: len(operands)], refs[len(operands)]
        refs = refs[len(operands) + 1 :]
        priors, refs = refs[: len(prior)], refs[len(prior) + len(after) :]
        out, pair, lhs, table_ref, result, in_sems, table_sem, prior_sem, out_sems = refs
        pick = role(lax.axis_index("tm")) if role is not None else None

        def copy(number, side, half, place):
            return pltpu.make_async_copy(
                cands[place].at[half],
                pair.at[number, half, :, :, pl.ds(side * near, near), :],
                in_sems.at[number, half, side],
            )

        for half in range(halves):
            for number, source in enumerate(layout):
                for side, places in enumerate(source):
                    if len(places) == 1:
                        copy(number, side, half, places[0]).start()
                        continue
                    for choice, place in enumerate(places):

                        @pl.when(pick == choice)
                        def _():
                            copy(number, side, half, place).start()

        table_copy = pltpu.make_async_copy(table_any, table_ref, table_sem)
        table_copy.start()
        if prior:
            prior_copy = pltpu.make_async_copy(priors[0], result, prior_sem)
            prior_copy.start()

        def each_half(half, _):
            for number, source in enumerate(layout):
                for side, places in enumerate(source):
                    copy(number, side, half, places[0]).wait()
                products(pair.at[number], half, lhs, groups, number == 0)
            return 0

        lax.fori_loop(0, halves, each_half, 0)
        table_copy.wait()
        if prior:
            prior_copy.wait()
        copies = []
        for begin in range(0, shape[0], chunk):
            size = min(chunk, shape[0] - begin)
            span = pl.ds(8 * begin, 8 * size)
            value = jnp.concatenate([lhs[half, span, :] for half in range(halves)], axis=1)
            lagged = dot_split(value, table_ref[...]).reshape(size, 8, LAGS)
            place = pl.ds(begin, size)
            result[place] = result[place] + lagged if prior else lagged
            copies.append(pltpu.make_async_copy(result.at[place], out.at[place], out_sems.at[len(copies)]))
            copies[-1].start()
        for done in copies:
            done.wait()

    far_memory = pl.BlockSpec(memory_space=pltpu.HBM)
    chunks = -(-shape[0] // chunk)
    return pl.pallas_call(
        kernel,
        in_specs=[far_memory] * (len(operands) + 1 + len(prior) + len(after)),
        out_specs=far_memory,
        out_shape=jax.ShapeDtypeStruct(shape, jnp.float32),
        scratch_shapes=[
            pltpu.VMEM((len(sources), halves, parts, segs, sides * near, lanes), jnp.float32),
            pltpu.VMEM((halves, rows, 2 * lanes), jnp.float32),
            pltpu.VMEM(table.shape, table.dtype),
            pltpu.VMEM(shape, jnp.float32),
            pltpu.SemaphoreType.DMA((len(sources), halves, 2)),
            pltpu.SemaphoreType.DMA,
            pltpu.SemaphoreType.DMA,
            pltpu.SemaphoreType.DMA((chunks,)),
        ],
        compiler_params=pltpu.CompilerParams(vmem_limit_bytes=VMEM_LIMIT),
        cost_estimate=pl.CostEstimate(flops=cost, bytes_accessed=1000, transcendentals=0),
        name="lag_" + which,
    )(*operands, table, *prior, *after)


def place(near, inside, across):
    count = len(inside)
    terms = [[term if isinstance(term, list) else [term] for term in kind] for kind in (inside, across)]
    operands = [value for kind in terms for term in kind for value, _ in term]
    kinds = ("inside", "across")
    parts = LAGS // LANES
    tiles = near // 8

    def kernel(*refs):
        given, refs = list(refs[: len(operands)]), refs[len(operands) :]
        sources = [[[(given.pop(0), begin) for _, begin in term] for term in kind] for kind in terms]
        out, buffers, (stage, in_sems, out_sems) = refs[0], refs[1:3], refs[3:]
        z = lax.axis_index("tm")
        end = (z == 0) | (z == 3)
        loads, groups = {}, {}
        for tile in range(tiles):
            for kind in range(2):
                known = groups_of(near, kinds[kind])
                mine = [index for index, group in enumerate(known) if group[0] == tile]
                groups[tile, kind] = [(index, known[index][1]) for index in mine]
                if not mine:
                    continue
                span = pl.ds(mine[0], len(mine))
                for term in range(count):
                    copies = [
                        pltpu.make_async_copy(
                            value.at[pl.ds(begin + mine[0], len(mine))],
                            buffers[kind].at[term, span],
                            in_sems.at[tile, kind, term],
                        )
                        for value, begin in sources[kind][term]
                    ]
                    loads[tile, kind, term] = copies[0]
                    if len(copies) == 1:
                        copies[0].start()
                    else:
                        pl.when(end)(copies[0].start)
                        pl.when(jnp.logical_not(end))(copies[1].start)
        stores = []
        for tile in range(tiles):
            for kind in range(2):
                for term in range(count):
                    if (tile, kind, term) in loads:
                        loads[tile, kind, term].wait()
                for index, offset in groups[tile, kind]:
                    value = buffers[kind][0, index]
                    for term in range(1, count):
                        value = value + buffers[kind][term, index]
                    for part in range(parts):
                        stage[part, pl.ds(8 * tile * near + offset - 1, 8, stride=near), :] = value[
                            :, LANES * part : LANES * part + LANES
                        ]
            for part in range(parts):
                stores.append(
                    pltpu.make_async_copy(
                        stage.at[part].reshape(near, near, LANES).at[pl.ds(8 * tile, 8)],
                        out.at[pl.ds(8 * tile, 8), :, pl.ds(LANES * part, LANES)],
                        out_sems.at[tile, part],
                    )
                )
                stores[-1].start()
        for store in stores:
            store.wait()

    far_memory = pl.BlockSpec(memory_space=pltpu.HBM)
    return pl.pallas_call(
        kernel,
        in_specs=[far_memory] * len(operands),
        out_specs=far_memory,
        out_shape=jax.ShapeDtypeStruct((near, near, LAGS), jnp.float32),
        scratch_shapes=[pltpu.VMEM((count, len(groups_of(near, kind)), 8, LAGS), jnp.float32) for kind in kinds]
        + [
            pltpu.VMEM((parts, near * near, LANES), jnp.float32),
            pltpu.SemaphoreType.DMA((tiles, 2, count)),
            pltpu.SemaphoreType.DMA((tiles, parts)),
        ],
        compiler_params=pltpu.CompilerParams(vmem_limit_bytes=VMEM_LIMIT),
        cost_estimate=pl.CostEstimate(flops=COST, bytes_accessed=1000, transcendentals=0),
        name="place",
    )(*operands)


def shifted(value, steps):
    count = lax.axis_size("fibre")
    return lax.ppermute(value, "fibre", [(source, source + steps) for source in range(max(0, -steps), count)])


def line_of_four(traces):
    channels, segs, win = traces.shape
    tables = make_tables(win, LAGS, segs * 4)
    blocks = traces.reshape(4, NEAR, segs, win)
    fibres = lax.axis_size("fibre")

    def outer(value):
        return lax.ppermute(value, "tm", [(0, 1), (3, 2)])

    def outer_next(value):
        pairs = [(4 * fibre + 4, 4 * fibre + 1) for fibre in range(fibres - 1)]
        pairs += [(4 * fibre + 3, 4 * fibre + 2) for fibre in range(fibres)]
        return lax.ppermute(value, ("fibre", "tm"), pairs)

    def middle(value):
        return lax.ppermute(value, "tm", [(1, 2), (2, 1)])

    def inner(value):
        return lax.ppermute(value, "tm", [(1, 0), (2, 3)])

    (far,) = whiten_first(blocks, tables)
    e1 = outer(far)
    *own, next_far, last = whiten_first(blocks, tables, far)
    e2 = outer_next(next_far)
    own.append(shifted(own[0], -1))
    e3 = outer(own[2])

    role = lambda z: jnp.where(z < 2, 0, 1)
    jobs = functools.partial(lag_sums, tables=tables, inner=True)
    back_in = jobs("inside", [([own[0], own[3]], None)], role=role, cost=1_000_000)
    m1 = jobs("inside", [([own[3], own[0]], None), ([e1], None)], role=role, after=[back_in])
    m1_in = middle(m1)
    base = jobs("across", [([own[3], own[0]], [own[4], own[1]])], role=role, after=[m1])
    m2 = jobs("across", [([e1], [e2])], prior=[base])
    m2_in = middle(m2)
    m1_in, _ = lax.optimization_barrier((m1_in, m2))
    first = m1_in + back_in
    i1 = inner(first)
    last, _ = lax.optimization_barrier((last, first))
    e4 = outer(last)
    m3 = jobs("all", [([own[2], own[1]], [own[3], own[2]]), ([e3, e2], [e1, e3])], role=role, after=[first])
    m3_in = middle(m3)
    second = jobs("across", [([own[0], own[3]], [own[1], own[4]])], role=role, prior=[m2_in], after=[m3])
    i2 = inner(second)
    near = lag_sums(
        "all", [(own[:4], own[1:]), ([e4, e4, e3, e4], [e3, e3, e4, e3])], tables, lambda z: z, after=[second]
    )
    start = m1.shape[0]
    return place(NEAR, [(near, 0), [(i1, 0), (m3_in, 0)]], [(near, start), [(i2, 0), (m3_in, start)]])


def any_line(traces):
    channels, segs, win = traces.shape
    tables = make_tables(win, LAGS, segs * lax.axis_size("tm"))
    count = channels // NEAR
    blocks = traces.reshape(count, NEAR, segs, win)
    halo = shifted(blocks[0], -1)
    spectra = whiten(blocks, tables, count) + whiten(halo[None], tables, 1)
    start = len(groups_of(NEAR, "inside"))
    pieces = []
    for index in range(count):
        sums = lag_sums("all", [([spectra[index]], [spectra[index + 1]])], tables)
        pieces.append(place(NEAR, [(sums, 0)], [(sums, start)]))
    return lax.psum_scatter(jnp.concatenate(pieces, axis=0), "tm", scatter_dimension=0, tiled=True)


def shards(traces):
    if lax.axis_size("tm") == 4 and traces.shape[0] == 4 * NEAR:
        return line_of_four(traces)
    return any_line(traces)


def solution(mesh):
    in_specs = (P("fibre", "tm", None),)
    out_specs = P(("fibre", "tm"), None, None)
    return jax.shard_map(shards, mesh=mesh, in_specs=in_specs, out_specs=out_specs, check_vma=False)
```

```python
import functools

import jax
import jax.numpy as jnp
import ml_dtypes
import numpy as np
from jax import lax
from jax.experimental import pallas as pl
from jax.experimental.pallas import tpu as pltpu
from jax.sharding import PartitionSpec as P

NEAR = 32
LAGS = 256
HALF = 8
LANES = 128
VMEM_LIMIT = 64 << 20
COST = 10_000_000_000


def split_table(table):
    high = table.astype(ml_dtypes.bfloat16)
    low = (table - high.astype(np.float64)).astype(ml_dtypes.bfloat16)
    return np.concatenate([high, low, high], axis=0)


def make_tables(win, lags, segs):
    bins = win // 2
    samples = np.arange(win)
    hann = 0.5 - 0.5 * np.cos(2.0 * np.pi * samples / win)
    even, odd = np.arange(2, bins + 1, 2), np.arange(1, bins, 2)
    order = np.concatenate([even, odd])

    def forward(picked):
        phases = 2.0 * np.pi * ((samples[: win // 2, None] * picked[None, :]) % win) / win
        return split_table(np.concatenate([np.cos(phases), -np.sin(phases)], axis=1))

    near = np.abs(order[:, None] - order[None, :]) <= HALF
    band = near / (2.0 * HALF + 1.0) + 0.1 / bins
    lag = np.arange(lags) - lags // 2
    phases = 2.0 * np.pi * ((order[:, None] * lag[None, :]) % win) / win
    rows = [part for half in np.split(phases, 2) for part in (np.cos(half), -np.sin(half))]
    return {
        "hann": np.tile(hann.astype(np.float32)[None, :], (8, 1)),
        "forward": np.stack([forward(even), forward(odd), split_table(band)]),
        "inverse": split_table(np.concatenate(rows, axis=0) / segs),
    }


def dot_split(value, table):
    high = value.astype(jnp.bfloat16)
    low = (value - high.astype(jnp.float32)).astype(jnp.bfloat16)
    return jnp.dot(jnp.concatenate([high, high, low], axis=1), table, preferred_element_type=jnp.float32)


def whiten_block(x_ref, hann, forward, w_ref, stage):
    channels, segs, win = x_ref.shape
    parts = win // LANES
    for part in range(parts):
        lanes = slice(LANES * part, LANES * part + LANES)
        stage[part, pl.ds(0, channels * segs)] = x_ref[:, :, lanes].reshape(channels * segs, LANES)
    pieces = []
    for s in range(segs):
        pieces.append([
            stage[part, pl.ds(s, channels, stride=segs), :] * hann[0:1, LANES * part : LANES * part + LANES]
            for part in range(parts)
        ])
    quarter = [jnp.concatenate([piece[part] for piece in pieces], axis=0) for part in range(parts)]
    both = jnp.concatenate([quarter[0] + quarter[2], quarter[1] + quarter[3]], axis=1)
    between = jnp.concatenate([quarter[0] - quarter[2], quarter[1] - quarter[3]], axis=1)
    spectra = (dot_split(both, forward[0]), dot_split(between, forward[1]))
    energy = jnp.concatenate(
        [sp[:, :LANES] * sp[:, :LANES] + sp[:, LANES:] * sp[:, LANES:] for sp in spectra], axis=1
    )
    scale = lax.rsqrt(dot_split(energy, forward[2]) + 1e-06)
    for half, sp in enumerate(spectra):
        own = scale[:, LANES * half : LANES * half + LANES]
        real, imag = sp[:, :LANES] * own, sp[:, LANES:] * own
        for s in range(segs):
            rows = slice(channels * s, channels * s + channels)
            w_ref[half, 0, s] = real[rows]
            w_ref[half, 1, s] = imag[rows]


def whiten(x, tables, count):
    near, segs, win = x.shape[1:]
    consts = [jnp.asarray(tables["hann"]), jnp.asarray(tables["forward"])]

    def kernel(*refs):
        x_any, hann_any, forward_any = refs[:3]
        outs, refs = refs[3 : 3 + count], refs[3 + count :]
        stage, hann, forward, blocks_in, blocks_out, sems, out_sems = refs
        loads = [pltpu.make_async_copy(x_any.at[b], blocks_in.at[b], sems.at[b]) for b in range(count)]
        tabs = [
            pltpu.make_async_copy(hann_any, hann, sems.at[count]),
            pltpu.make_async_copy(forward_any, forward, sems.at[count + 1]),
        ]
        for load in tabs + loads:
            load.start()
        for load in tabs:
            load.wait()
        stores = []
        for index in range(count):
            loads[index].wait()
            whiten_block(blocks_in.at[index], hann, forward, blocks_out.at[index], stage)
            stores.append(pltpu.make_async_copy(blocks_out.at[index], outs[index], out_sems.at[index]))
            stores[-1].start()
        for store in stores:
            store.wait()

    shape = (2, 2, segs, near, LANES)
    far_memory = pl.BlockSpec(memory_space=pltpu.HBM)
    return pl.pallas_call(
        kernel,
        in_specs=[far_memory] * 3,
        out_specs=[far_memory] * count,
        out_shape=[jax.ShapeDtypeStruct(shape, jnp.float32)] * count,
        scratch_shapes=[
            pltpu.VMEM((win // LANES, near * segs, LANES), jnp.float32),
            pltpu.VMEM(consts[0].shape, consts[0].dtype),
            pltpu.VMEM(consts[1].shape, consts[1].dtype),
            pltpu.VMEM((count, near, segs, win), jnp.float32),
            pltpu.VMEM((count,) + shape, jnp.float32),
            pltpu.SemaphoreType.DMA((count + 2,)),
            pltpu.SemaphoreType.DMA((count,)),
        ],
        compiler_params=pltpu.CompilerParams(vmem_limit_bytes=VMEM_LIMIT),
        cost_estimate=pl.CostEstimate(flops=COST, bytes_accessed=1000, transcendentals=0),
        name="whiten",
    )(x, *consts)


def take_far(x):
    chunks = 4
    step = x.shape[1] // chunks

    def kernel(x_any, out, held, in_sems, out_sems):
        z = lax.axis_index("tm")

        @pl.when((z == 0) | (z == 3))
        def _():
            place = jnp.where(z < 2, 3, 0)
            spans = [pl.ds(step * chunk, step) for chunk in range(chunks)]
            loads = [
                pltpu.make_async_copy(x_any.at[place, span], held.at[span], in_sems.at[chunk])
                for chunk, span in enumerate(spans)
            ]
            stores = [
                pltpu.make_async_copy(held.at[span], out.at[span], out_sems.at[chunk])
                for chunk, span in enumerate(spans)
            ]
            for load in loads:
                load.start()
            for load, store in zip(loads, stores):
                load.wait()
                store.start()
            for store in stores:
                store.wait()

    far_memory = pl.BlockSpec(memory_space=pltpu.HBM)
    return pl.pallas_call(
        kernel,
        in_specs=[far_memory],
        out_specs=far_memory,
        out_shape=jax.ShapeDtypeStruct(x.shape[1:], jnp.float32),
        scratch_shapes=[
            pltpu.VMEM(x.shape[1:], jnp.float32),
            pltpu.SemaphoreType.DMA((chunks,)),
            pltpu.SemaphoreType.DMA((chunks,)),
        ],
        compiler_params=pltpu.CompilerParams(vmem_limit_bytes=VMEM_LIMIT),
        cost_estimate=pl.CostEstimate(flops=COST, bytes_accessed=1000, transcendentals=0),
        name="take_far",
    )(x)


def whiten_own(x, tables, after):
    near, segs, win = x.shape[1:]
    consts = [jnp.asarray(tables["hann"]), jnp.asarray(tables["forward"])]
    copies = ((0, 1), (1, 3))

    def kernel(x_any, hann_any, forward_any, _, *refs):
        outs, (stage, hann, forward, blocks_in, blocks_out, sems, out_sems) = refs[:6], refs[6:]
        z = lax.axis_index("tm")
        loads = [pltpu.make_async_copy(x_any.at[b], blocks_in.at[b], sems.at[b]) for b in range(4)]
        tabs = [
            pltpu.make_async_copy(hann_any, hann, sems.at[4]),
            pltpu.make_async_copy(forward_any, forward, sems.at[5]),
        ]
        for load in loads[:1] + tabs + loads[1:]:
            load.start()
        for tab in tabs:
            tab.wait()
        stores = []
        for b in range(4):
            loads[b].wait()
            whiten_block(blocks_in.at[b], hann, forward, blocks_out.at[b], stage)
            stores.append(pltpu.make_async_copy(blocks_out.at[b], outs[b], out_sems.at[b]))
            stores[-1].start()
        for at, sources in enumerate(copies):
            for side, source in enumerate(sources):

                @pl.when(z < 2 if side == 0 else z >= 2)
                def _():
                    pltpu.make_async_copy(blocks_out.at[source], outs[4 + at], out_sems.at[4 + at]).start()

            stores.append(pltpu.make_async_copy(blocks_out.at[sources[0]], outs[4 + at], out_sems.at[4 + at]))
        for store in stores:
            store.wait()

    shape = (2, 2, segs, near, LANES)
    far_memory = pl.BlockSpec(memory_space=pltpu.HBM)
    return pl.pallas_call(
        kernel,
        in_specs=[far_memory] * 4,
        out_specs=[far_memory] * 6,
        out_shape=[jax.ShapeDtypeStruct(shape, jnp.float32)] * 6,
        scratch_shapes=[
            pltpu.VMEM((win // LANES, near * segs, LANES), jnp.float32),
            pltpu.VMEM(consts[0].shape, consts[0].dtype),
            pltpu.VMEM(consts[1].shape, consts[1].dtype),
            pltpu.VMEM((4, near, segs, win), jnp.float32),
            pltpu.VMEM((4,) + shape, jnp.float32),
            pltpu.SemaphoreType.DMA((6,)),
            pltpu.SemaphoreType.DMA((6,)),
        ],
        compiler_params=pltpu.CompilerParams(vmem_limit_bytes=VMEM_LIMIT),
        cost_estimate=pl.CostEstimate(flops=COST, bytes_accessed=1000, transcendentals=0),
        name="whiten_own",
    )(x, *consts, after)


def groups_of(near, which):
    tiles = near // 8
    inside = [(tile, offset) for tile in range(tiles) for offset in range(1, near - 8 * tile - 7)]
    across = [(tile, offset) for tile in range(tiles) for offset in range(near - 8 * tile - 7, near + 1)]
    return {"inside": inside, "across": across, "all": inside + across}[which]


def products(pair, half, lhs, groups, fresh, batch=4):
    segs = pair.shape[2]
    index_of = {group: index for index, group in enumerate(groups)}
    tiles = sorted({tile for tile, _ in groups})
    for begin in range(0, segs, batch):
        span = range(begin, min(begin + batch, segs))
        real = {t: [pair[half, 0, s, pl.ds(8 * t, 8), :] for s in span] for t in tiles}
        imag = {t: [pair[half, 1, s, pl.ds(8 * t, 8), :] for s in span] for t in tiles}
        added = {t: [re + im for re, im in zip(real[t], imag[t])] for t in tiles}
        for row in range(1, 8 * len(tiles) + NEAR):
            units = [(t, row - 8 * t) for t in tiles if (t, row - 8 * t) in index_of]
            if not units:
                continue
            sums = {}
            for at, s in enumerate(span):
                other_re = pair[half, 0, s, pl.ds(row, 8), :]
                other_im = pair[half, 1, s, pl.ds(row, 8), :]
                apart = other_re - other_im
                for unit in units:
                    t = unit[0]
                    terms = (real[t][at] * other_re, imag[t][at] * other_im, added[t][at] * apart)
                    sums[unit] = terms if at == 0 else tuple(old + new for old, new in zip(sums[unit], terms))
            for unit in units:
                rr, ii, mixed = sums[unit]
                cross_re, cross_im = rr + ii, mixed - rr + ii
                rows = pl.ds(8 * index_of[unit], 8)
                if not (fresh and begin == 0):
                    cross_re = cross_re + lhs[half, rows, :LANES]
                    cross_im = cross_im + lhs[half, rows, LANES:]
                lhs[half, rows, :LANES] = cross_re
                lhs[half, rows, LANES:] = cross_im


def lag_sums(which, sources, tables, role=None, prior=(), after=(), cost=COST, inner=False, raw=None):
    table = jnp.asarray(tables["inverse"])
    sample = sources[0][0][0]
    halves, parts, segs, near, lanes = sample.shape
    groups = groups_of(near, which)
    sides = 1 if which == "inside" else 2
    operands, layout = [], []
    for source in sources:
        layout.append([])
        for side in range(sides):
            places = []
            for value in source[side]:
                known = [i for i, other in enumerate(operands) if other is value]
                if not known:
                    operands.append(value)
                places.append(known[0] if known else len(operands) - 1)
            layout[-1].append(places)
    shape = (len(groups), 8, LAGS)
    total = len(sources) + (raw is not None)
    extras = [] if raw is None else [raw, jnp.asarray(tables["hann"]), jnp.asarray(tables["forward"])]
    rows = 8 * len(groups)
    chunk = 16

    def kernel(*refs):
        if not inner:
            return work(*refs)
        z = lax.axis_index("tm")
        pl.when((z == 1) | (z == 2))(lambda: work(*refs))

    def work(*refs):
        cands, table_any = refs[: len(operands)], refs[len(operands)]
        refs = refs[len(operands) + 1 :]
        priors, refs = refs[: len(prior)], refs[len(prior) + len(after) :]
        samples, refs = refs[: len(extras)], refs[len(extras) :]
        out, refs = refs[0], refs[1:]
        if raw is not None:
            white, refs = refs[0], refs[1:]
        pair, lhs, table_ref, result, in_sems, table_sem, prior_sem, out_sems = refs[:8]
        if raw is not None:
            stage, raw_sems = refs[8], refs[-1]
            held = refs[9:-1]
            raw_copies = [
                pltpu.make_async_copy(source, place, raw_sems.at[index])
                for index, (source, place) in enumerate(zip(samples, held))
            ]
            for raw_copy in raw_copies:
                raw_copy.start()
        pick = role(lax.axis_index("tm")) if role is not None else None

        def copy(number, side, half, place):
            return pltpu.make_async_copy(
                cands[place].at[half],
                pair.at[number, half, :, :, pl.ds(side * near, near), :],
                in_sems.at[number, half, side],
            )

        for half in range(halves):
            for number, source in enumerate(layout):
                for side, places in enumerate(source):
                    if len(places) == 1:
                        copy(number, side, half, places[0]).start()
                        continue
                    for choice, place in enumerate(places):

                        @pl.when(pick == choice)
                        def _():
                            copy(number, side, half, place).start()

        table_copy = pltpu.make_async_copy(table_any, table_ref, table_sem)
        table_copy.start()
        if prior:
            prior_copy = pltpu.make_async_copy(priors[0], result, prior_sem)
            prior_copy.start()

        if raw is not None:
            for raw_copy in raw_copies:
                raw_copy.wait()
            whiten_block(held[0], held[1], held[2], pair.at[total - 1], stage)
            white_copy = pltpu.make_async_copy(pair.at[total - 1], white, raw_sems.at[len(extras)])
            white_copy.start()

        def each_half(half, _):
            for number, source in enumerate(layout):
                for side, places in enumerate(source):
                    copy(number, side, half, places[0]).wait()
                products(pair.at[number], half, lhs, groups, number == 0)
            if raw is not None:
                products(pair.at[total - 1], half, lhs, groups, False)
            return 0

        lax.fori_loop(0, halves, each_half, 0)
        table_copy.wait()
        if prior:
            prior_copy.wait()
        copies = []
        for begin in range(0, shape[0], chunk):
            size = min(chunk, shape[0] - begin)
            span = pl.ds(8 * begin, 8 * size)
            value = jnp.concatenate([lhs[half, span, :] for half in range(halves)], axis=1)
            lagged = dot_split(value, table_ref[...]).reshape(size, 8, LAGS)
            place = pl.ds(begin, size)
            result[place] = result[place] + lagged if prior else lagged
            copies.append(pltpu.make_async_copy(result.at[place], out.at[place], out_sems.at[len(copies)]))
            copies[-1].start()
        for done in copies:
            done.wait()
        if raw is not None:
            white_copy.wait()

    far_memory = pl.BlockSpec(memory_space=pltpu.HBM)
    chunks = -(-shape[0] // chunk)
    results, spare = [jax.ShapeDtypeStruct(shape, jnp.float32)], []
    if raw is not None:
        results.append(jax.ShapeDtypeStruct(sample.shape, jnp.float32))
        spare = [pltpu.VMEM((raw.shape[2] // LANES, near * segs, LANES), jnp.float32)]
        spare += [pltpu.VMEM(value.shape, value.dtype) for value in extras]
        spare.append(pltpu.SemaphoreType.DMA((len(extras) + 1,)))
    outputs = pl.pallas_call(
        kernel,
        in_specs=[far_memory] * (len(operands) + 1 + len(prior) + len(after) + len(extras)),
        out_specs=[far_memory] * len(results),
        out_shape=results,
        scratch_shapes=[
            pltpu.VMEM((total, halves, parts, segs, sides * near, lanes), jnp.float32),
            pltpu.VMEM((halves, rows, 2 * lanes), jnp.float32),
            pltpu.VMEM(table.shape, table.dtype),
            pltpu.VMEM(shape, jnp.float32),
            pltpu.SemaphoreType.DMA((len(sources), halves, 2)),
            pltpu.SemaphoreType.DMA,
            pltpu.SemaphoreType.DMA,
            pltpu.SemaphoreType.DMA((chunks,)),
        ]
        + spare,
        compiler_params=pltpu.CompilerParams(vmem_limit_bytes=VMEM_LIMIT),
        cost_estimate=pl.CostEstimate(flops=cost, bytes_accessed=1000, transcendentals=0),
        name="lag_" + which,
    )(*operands, table, *prior, *after, *extras)
    return outputs[0] if raw is None else outputs


def place(near, inside, across):
    count = len(inside)
    terms = [[term if isinstance(term, list) else [term] for term in kind] for kind in (inside, across)]
    operands = [value for kind in terms for term in kind for value, _ in term]
    kinds = ("inside", "across")
    parts = LAGS // LANES
    tiles = near // 8

    def kernel(*refs):
        given, refs = list(refs[: len(operands)]), refs[len(operands) :]
        sources = [[[(given.pop(0), begin) for _, begin in term] for term in kind] for kind in terms]
        out, buffers, (stage, in_sems, out_sems) = refs[0], refs[1:3], refs[3:]
        z = lax.axis_index("tm")
        end = (z == 0) | (z == 3)
        loads, groups = {}, {}
        for tile in range(tiles):
            for kind in range(2):
                known = groups_of(near, kinds[kind])
                mine = [index for index, group in enumerate(known) if group[0] == tile]
                groups[tile, kind] = [(index, known[index][1]) for index in mine]
                if not mine:
                    continue
                span = pl.ds(mine[0], len(mine))
                for term in range(count):
                    copies = [
                        pltpu.make_async_copy(
                            value.at[pl.ds(begin + mine[0], len(mine))],
                            buffers[kind].at[term, span],
                            in_sems.at[tile, kind, term],
                        )
                        for value, begin in sources[kind][term]
                    ]
                    loads[tile, kind, term] = copies[0]
                    if len(copies) == 1:
                        copies[0].start()
                    else:
                        pl.when(end)(copies[0].start)
                        pl.when(jnp.logical_not(end))(copies[1].start)
        stores = []
        for tile in range(tiles):
            for kind in range(2):
                for term in range(count):
                    if (tile, kind, term) in loads:
                        loads[tile, kind, term].wait()
                for index, offset in groups[tile, kind]:
                    value = buffers[kind][0, index]
                    for term in range(1, count):
                        value = value + buffers[kind][term, index]
                    for part in range(parts):
                        stage[part, pl.ds(8 * tile * near + offset - 1, 8, stride=near), :] = value[
                            :, LANES * part : LANES * part + LANES
                        ]
            for part in range(parts):
                stores.append(
                    pltpu.make_async_copy(
                        stage.at[part].reshape(near, near, LANES).at[pl.ds(8 * tile, 8)],
                        out.at[pl.ds(8 * tile, 8), :, pl.ds(LANES * part, LANES)],
                        out_sems.at[tile, part],
                    )
                )
                stores[-1].start()
        for store in stores:
            store.wait()

    far_memory = pl.BlockSpec(memory_space=pltpu.HBM)
    return pl.pallas_call(
        kernel,
        in_specs=[far_memory] * len(operands),
        out_specs=far_memory,
        out_shape=jax.ShapeDtypeStruct((near, near, LAGS), jnp.float32),
        scratch_shapes=[pltpu.VMEM((count, len(groups_of(near, kind)), 8, LAGS), jnp.float32) for kind in kinds]
        + [
            pltpu.VMEM((parts, near * near, LANES), jnp.float32),
            pltpu.SemaphoreType.DMA((tiles, 2, count)),
            pltpu.SemaphoreType.DMA((tiles, parts)),
        ],
        compiler_params=pltpu.CompilerParams(vmem_limit_bytes=VMEM_LIMIT),
        cost_estimate=pl.CostEstimate(flops=COST, bytes_accessed=1000, transcendentals=0),
        name="place",
    )(*operands)


def shifted(value, steps):
    count = lax.axis_size("fibre")
    return lax.ppermute(value, "fibre", [(source, source + steps) for source in range(max(0, -steps), count)])


def line_of_four(traces):
    channels, segs, win = traces.shape
    tables = make_tables(win, LAGS, segs * 4)
    blocks = traces.reshape(4, NEAR, segs, win)
    fibres = lax.axis_size("fibre")

    def outer(value):
        return lax.ppermute(value, "tm", [(0, 1), (3, 2)])

    def outer_next(value):
        pairs = [(4 * fibre + 4, 4 * fibre + 1) for fibre in range(fibres - 1)]
        pairs += [(4 * fibre + 3, 4 * fibre + 2) for fibre in range(fibres)]
        return lax.ppermute(value, ("fibre", "tm"), pairs)

    def middle(value):
        return lax.ppermute(value, "tm", [(1, 2), (2, 1)])

    def inner(value):
        return lax.ppermute(value, "tm", [(1, 0), (2, 3)])

    far = take_far(blocks)
    e1 = outer(far)
    *own, next_far, last = whiten_own(blocks, tables, far)
    e2 = outer_next(next_far)
    own.append(shifted(own[0], -1))
    e3 = outer(own[2])

    role = lambda z: jnp.where(z < 2, 0, 1)
    jobs = functools.partial(lag_sums, tables=tables, inner=True)
    back_in = jobs("inside", [([own[0], own[3]], None)], role=role, cost=1_000_000)
    m1, e1 = jobs("inside", [([own[3], own[0]], None)], role=role, after=[back_in], raw=e1)
    m1_in = middle(m1)
    base = jobs("across", [([own[3], own[0]], [own[4], own[1]])], role=role, after=[m1])
    m2 = jobs("across", [([e1], [e2])], prior=[base])
    m2_in = middle(m2)
    m1_in, _ = lax.optimization_barrier((m1_in, m2))
    first = m1_in + back_in
    i1 = inner(first)
    last, _ = lax.optimization_barrier((last, first))
    e4 = outer(last)
    m3 = jobs("all", [([own[2], own[1]], [own[3], own[2]]), ([e3, e2], [e1, e3])], role=role, after=[first])
    m3_in = middle(m3)
    second = jobs("across", [([own[0], own[3]], [own[1], own[4]])], role=role, prior=[m2_in], after=[m3])
    i2 = inner(second)
    near = lag_sums(
        "all", [(own[:4], own[1:]), ([e4, e4, e3, e4], [e3, e3, e4, e3])], tables, lambda z: z, after=[second]
    )
    start = m1.shape[0]
    return place(NEAR, [(near, 0), [(i1, 0), (m3_in, 0)]], [(near, start), [(i2, 0), (m3_in, start)]])


def any_line(traces):
    channels, segs, win = traces.shape
    tables = make_tables(win, LAGS, segs * lax.axis_size("tm"))
    count = channels // NEAR
    blocks = traces.reshape(count, NEAR, segs, win)
    halo = shifted(blocks[0], -1)
    spectra = whiten(blocks, tables, count) + whiten(halo[None], tables, 1)
    start = len(groups_of(NEAR, "inside"))
    pieces = []
    for index in range(count):
        sums = lag_sums("all", [([spectra[index]], [spectra[index + 1]])], tables)
        pieces.append(place(NEAR, [(sums, 0)], [(sums, start)]))
    return lax.psum_scatter(jnp.concatenate(pieces, axis=0), "tm", scatter_dimension=0, tiled=True)


def shards(traces):
    if lax.axis_size("tm") == 4 and traces.shape[0] == 4 * NEAR:
        return line_of_four(traces)
    return any_line(traces)


def solution(mesh):
    in_specs = (P("fibre", "tm", None),)
    out_specs = P(("fibre", "tm"), None, None)
    return jax.shard_map(shards, mesh=mesh, in_specs=in_specs, out_specs=out_specs, check_vma=False)
```

```python
import functools

import jax
import jax.numpy as jnp
import ml_dtypes
import numpy as np
from jax import lax
from jax.experimental import pallas as pl
from jax.experimental.pallas import tpu as pltpu
from jax.sharding import PartitionSpec as P

NEAR = 32
LAGS = 256
HALF = 8
LANES = 128
VMEM_LIMIT = 64 << 20
COST = 10_000_000_000


def split_table(table):
    high = table.astype(ml_dtypes.bfloat16)
    low = (table - high.astype(np.float64)).astype(ml_dtypes.bfloat16)
    return np.concatenate([high, low], axis=0)


def make_tables(win, lags, segs):
    bins = win // 2
    samples = np.arange(win)
    hann = 0.5 - 0.5 * np.cos(2.0 * np.pi * samples / win)
    even, odd = np.arange(2, bins + 1, 2), np.arange(1, bins, 2)
    order = np.concatenate([even, odd])

    def forward(picked):
        phases = 2.0 * np.pi * ((samples[: win // 2, None] * picked[None, :]) % win) / win
        return split_table(np.concatenate([np.cos(phases), -np.sin(phases)], axis=1))

    near = np.abs(order[:, None] - order[None, :]) <= HALF
    band = near / (2.0 * HALF + 1.0) + 0.1 / bins
    lag = np.arange(lags) - lags // 2
    phases = 2.0 * np.pi * ((order[:, None] * lag[None, :]) % win) / win
    rows = [part for half in np.split(phases, 2) for part in (np.cos(half), -np.sin(half))]
    return {
        "hann": np.tile(hann.astype(np.float32)[None, :], (8, 1)),
        "forward": np.stack([forward(even), forward(odd), split_table(band)]),
        "inverse": split_table(np.concatenate(rows, axis=0) / segs),
    }


def dot_split(value, table):
    high = value.astype(jnp.bfloat16)
    low = (value - high.astype(jnp.float32)).astype(jnp.bfloat16)
    dot = functools.partial(jnp.dot, preferred_element_type=jnp.float32)
    return dot(jnp.concatenate([high, high], axis=1), table[...]) + dot(low, table[: value.shape[1]])


def whiten_block(x_ref, hann, forward, w_ref, stage):
    channels, segs, win = x_ref.shape
    parts = win // LANES
    for part in range(parts):
        lanes = slice(LANES * part, LANES * part + LANES)
        stage[part, pl.ds(0, channels * segs)] = x_ref[:, :, lanes].reshape(channels * segs, LANES)
    pieces = []
    for s in range(segs):
        pieces.append([
            stage[part, pl.ds(s, channels, stride=segs), :] * hann[0:1, LANES * part : LANES * part + LANES]
            for part in range(parts)
        ])
    quarter = [jnp.concatenate([piece[part] for piece in pieces], axis=0) for part in range(parts)]
    both = jnp.concatenate([quarter[0] + quarter[2], quarter[1] + quarter[3]], axis=1)
    between = jnp.concatenate([quarter[0] - quarter[2], quarter[1] - quarter[3]], axis=1)
    spectra = (dot_split(both, forward.at[0]), dot_split(between, forward.at[1]))
    energy = jnp.concatenate(
        [sp[:, :LANES] * sp[:, :LANES] + sp[:, LANES:] * sp[:, LANES:] for sp in spectra], axis=1
    )
    scale = lax.rsqrt(dot_split(energy, forward.at[2]) + 1e-06)
    for half, sp in enumerate(spectra):
        own = scale[:, LANES * half : LANES * half + LANES]
        real, imag = sp[:, :LANES] * own, sp[:, LANES:] * own
        for s in range(segs):
            rows = slice(channels * s, channels * s + channels)
            w_ref[half, 0, s] = real[rows]
            w_ref[half, 1, s] = imag[rows]


def whiten(x, tables, count):
    near, segs, win = x.shape[1:]
    consts = [jnp.asarray(tables["hann"]), jnp.asarray(tables["forward"])]

    def kernel(*refs):
        x_any, hann_any, forward_any = refs[:3]
        outs, refs = refs[3 : 3 + count], refs[3 + count :]
        stage, hann, forward, blocks_in, blocks_out, sems, out_sems = refs
        loads = [pltpu.make_async_copy(x_any.at[b], blocks_in.at[b], sems.at[b]) for b in range(count)]
        tabs = [
            pltpu.make_async_copy(hann_any, hann, sems.at[count]),
            pltpu.make_async_copy(forward_any, forward, sems.at[count + 1]),
        ]
        for load in tabs + loads:
            load.start()
        for load in tabs:
            load.wait()
        stores = []
        for index in range(count):
            loads[index].wait()
            whiten_block(blocks_in.at[index], hann, forward, blocks_out.at[index], stage)
            stores.append(pltpu.make_async_copy(blocks_out.at[index], outs[index], out_sems.at[index]))
            stores[-1].start()
        for store in stores:
            store.wait()

    shape = (2, 2, segs, near, LANES)
    far_memory = pl.BlockSpec(memory_space=pltpu.HBM)
    return pl.pallas_call(
        kernel,
        in_specs=[far_memory] * 3,
        out_specs=[far_memory] * count,
        out_shape=[jax.ShapeDtypeStruct(shape, jnp.float32)] * count,
        scratch_shapes=[
            pltpu.VMEM((win // LANES, near * segs + segs, LANES), jnp.float32),
            pltpu.VMEM(consts[0].shape, consts[0].dtype),
            pltpu.VMEM(consts[1].shape, consts[1].dtype),
            pltpu.VMEM((count, near, segs, win), jnp.float32),
            pltpu.VMEM((count,) + shape, jnp.float32),
            pltpu.SemaphoreType.DMA((count + 2,)),
            pltpu.SemaphoreType.DMA((count,)),
        ],
        compiler_params=pltpu.CompilerParams(vmem_limit_bytes=VMEM_LIMIT),
        cost_estimate=pl.CostEstimate(flops=COST, bytes_accessed=1000, transcendentals=0),
        name="whiten",
    )(x, *consts)


def take_far(x):
    chunks = 4
    step = x.shape[1] // chunks

    def kernel(x_any, out, held, in_sems, out_sems):
        z = lax.axis_index("tm")

        @pl.when((z == 0) | (z == 3))
        def _():
            place = jnp.where(z < 2, 3, 0)
            spans = [pl.ds(step * chunk, step) for chunk in range(chunks)]
            loads = [
                pltpu.make_async_copy(x_any.at[place, span], held.at[span], in_sems.at[chunk])
                for chunk, span in enumerate(spans)
            ]
            stores = [
                pltpu.make_async_copy(held.at[span], out.at[span], out_sems.at[chunk])
                for chunk, span in enumerate(spans)
            ]
            for load in loads:
                load.start()
            for load, store in zip(loads, stores):
                load.wait()
                store.start()
            for store in stores:
                store.wait()

    far_memory = pl.BlockSpec(memory_space=pltpu.HBM)
    return pl.pallas_call(
        kernel,
        in_specs=[far_memory],
        out_specs=far_memory,
        out_shape=jax.ShapeDtypeStruct(x.shape[1:], jnp.float32),
        scratch_shapes=[
            pltpu.VMEM(x.shape[1:], jnp.float32),
            pltpu.SemaphoreType.DMA((chunks,)),
            pltpu.SemaphoreType.DMA((chunks,)),
        ],
        compiler_params=pltpu.CompilerParams(vmem_limit_bytes=VMEM_LIMIT),
        cost_estimate=pl.CostEstimate(flops=COST, bytes_accessed=1000, transcendentals=0),
        name="take_far",
    )(x)


def whiten_own(x, tables, after):
    near, segs, win = x.shape[1:]
    consts = [jnp.asarray(tables["hann"]), jnp.asarray(tables["forward"])]
    copies = ((0, 1), (1, 3))

    def kernel(x_any, hann_any, forward_any, _, *refs):
        outs, (stage, hann, forward, blocks_in, blocks_out, sems, out_sems) = refs[:6], refs[6:]
        z = lax.axis_index("tm")
        loads = [pltpu.make_async_copy(x_any.at[b], blocks_in.at[b], sems.at[b]) for b in range(4)]
        tabs = [
            pltpu.make_async_copy(hann_any, hann, sems.at[4]),
            pltpu.make_async_copy(forward_any, forward, sems.at[5]),
        ]
        for load in loads[:1] + tabs + loads[1:]:
            load.start()
        for tab in tabs:
            tab.wait()
        stores = []
        for b in range(4):
            loads[b].wait()
            whiten_block(blocks_in.at[b], hann, forward, blocks_out.at[b], stage)
            stores.append(pltpu.make_async_copy(blocks_out.at[b], outs[b], out_sems.at[b]))
            stores[-1].start()
        for at, sources in enumerate(copies):
            for side, source in enumerate(sources):

                @pl.when(z < 2 if side == 0 else z >= 2)
                def _():
                    pltpu.make_async_copy(blocks_out.at[source], outs[4 + at], out_sems.at[4 + at]).start()

            stores.append(pltpu.make_async_copy(blocks_out.at[sources[0]], outs[4 + at], out_sems.at[4 + at]))
        for store in stores:
            store.wait()

    shape = (2, 2, segs, near, LANES)
    far_memory = pl.BlockSpec(memory_space=pltpu.HBM)
    return pl.pallas_call(
        kernel,
        in_specs=[far_memory] * 4,
        out_specs=[far_memory] * 6,
        out_shape=[jax.ShapeDtypeStruct(shape, jnp.float32)] * 6,
        scratch_shapes=[
            pltpu.VMEM((win // LANES, near * segs + segs, LANES), jnp.float32),
            pltpu.VMEM(consts[0].shape, consts[0].dtype),
            pltpu.VMEM(consts[1].shape, consts[1].dtype),
            pltpu.VMEM((4, near, segs, win), jnp.float32),
            pltpu.VMEM((4,) + shape, jnp.float32),
            pltpu.SemaphoreType.DMA((6,)),
            pltpu.SemaphoreType.DMA((6,)),
        ],
        compiler_params=pltpu.CompilerParams(vmem_limit_bytes=VMEM_LIMIT),
        cost_estimate=pl.CostEstimate(flops=COST, bytes_accessed=1000, transcendentals=0),
        name="whiten_own",
    )(x, *consts, after)


def groups_of(near, which):
    tiles = near // 8
    inside = [(tile, offset) for tile in range(tiles) for offset in range(1, near - 8 * tile - 7)]
    across = [(tile, offset) for tile in range(tiles) for offset in range(near - 8 * tile - 7, near + 1)]
    return {"inside": inside, "across": across, "all": inside + across}[which]


def products(pair, half, lhs, groups, fresh, batch=4):
    segs = pair.shape[2]
    index_of = {group: index for index, group in enumerate(groups)}
    tiles = sorted({tile for tile, _ in groups})
    for begin in range(0, segs, batch):
        span = range(begin, min(begin + batch, segs))
        real = {t: [pair[half, 0, s, pl.ds(8 * t, 8), :] for s in span] for t in tiles}
        imag = {t: [pair[half, 1, s, pl.ds(8 * t, 8), :] for s in span] for t in tiles}
        added = {t: [re + im for re, im in zip(real[t], imag[t])] for t in tiles}
        for row in range(1, 8 * len(tiles) + NEAR):
            units = [(t, row - 8 * t) for t in tiles if (t, row - 8 * t) in index_of]
            if not units:
                continue
            sums = {}
            for at, s in enumerate(span):
                other_re = pair[half, 0, s, pl.ds(row, 8), :]
                other_im = pair[half, 1, s, pl.ds(row, 8), :]
                apart = other_re - other_im
                for unit in units:
                    t = unit[0]
                    terms = (real[t][at] * other_re, imag[t][at] * other_im, added[t][at] * apart)
                    sums[unit] = terms if at == 0 else tuple(old + new for old, new in zip(sums[unit], terms))
            for unit in units:
                rr, ii, mixed = sums[unit]
                cross_re, cross_im = rr + ii, mixed - rr + ii
                rows = pl.ds(8 * index_of[unit], 8)
                if not (fresh and begin == 0):
                    cross_re = cross_re + lhs[half, rows, :LANES]
                    cross_im = cross_im + lhs[half, rows, LANES:]
                lhs[half, rows, :LANES] = cross_re
                lhs[half, rows, LANES:] = cross_im


def lag_sums(which, sources, tables, role=None, prior=(), after=(), cost=COST, inner=False, raw=None):
    table = jnp.asarray(tables["inverse"])
    sample = sources[0][0][0]
    halves, parts, segs, near, lanes = sample.shape
    groups = groups_of(near, which)
    sides = 1 if which == "inside" else 2
    operands, layout = [], []
    for source in sources:
        layout.append([])
        for side in range(sides):
            places = []
            for value in source[side]:
                known = [i for i, other in enumerate(operands) if other is value]
                if not known:
                    operands.append(value)
                places.append(known[0] if known else len(operands) - 1)
            layout[-1].append(places)
    shape = (len(groups), 8, LAGS)
    total = len(sources) + (raw is not None)
    extras = [] if raw is None else [raw, jnp.asarray(tables["hann"]), jnp.asarray(tables["forward"])]
    rows = 8 * len(groups)
    chunk = 16

    def kernel(*refs):
        if not inner:
            return work(*refs)
        z = lax.axis_index("tm")
        pl.when((z == 1) | (z == 2))(lambda: work(*refs))

    def work(*refs):
        cands, table_any = refs[: len(operands)], refs[len(operands)]
        refs = refs[len(operands) + 1 :]
        priors, refs = refs[: len(prior)], refs[len(prior) + len(after) :]
        samples, refs = refs[: len(extras)], refs[len(extras) :]
        out, refs = refs[0], refs[1:]
        if raw is not None:
            white, refs = refs[0], refs[1:]
        pair, lhs, table_ref, result, in_sems, table_sem, prior_sem, out_sems = refs[:8]
        if raw is not None:
            stage, raw_sems = refs[8], refs[-1]
            held = refs[9:-1]
            raw_copies = [
                pltpu.make_async_copy(source, place, raw_sems.at[index])
                for index, (source, place) in enumerate(zip(samples, held))
            ]
        pick = role(lax.axis_index("tm")) if role is not None else None

        def copy(number, side, half, place):
            return pltpu.make_async_copy(
                cands[place].at[half],
                pair.at[number, half, :, :, pl.ds(side * near, near), :],
                in_sems.at[number, half, side],
            )

        for half in range(halves):
            for number, source in enumerate(layout):
                for side, places in enumerate(source):
                    if len(places) == 1:
                        copy(number, side, half, places[0]).start()
                        continue
                    for choice, place in enumerate(places):

                        @pl.when(pick == choice)
                        def _():
                            copy(number, side, half, place).start()

        if raw is not None:
            for raw_copy in raw_copies:
                raw_copy.start()
        table_copy = pltpu.make_async_copy(table_any, table_ref, table_sem)
        table_copy.start()
        if prior:
            prior_copy = pltpu.make_async_copy(priors[0], result, prior_sem)
            prior_copy.start()

        def each_half(half, _):
            for number, source in enumerate(layout):
                for side, places in enumerate(source):
                    copy(number, side, half, places[0]).wait()
                products(pair.at[number], half, lhs, groups, number == 0)
            return 0

        def each_raw_half(half, _):
            products(pair.at[total - 1], half, lhs, groups, False)
            return 0

        lax.fori_loop(0, halves, each_half, 0)
        if raw is not None:
            for raw_copy in raw_copies:
                raw_copy.wait()
            whiten_block(held[0], held[1], held[2], pair.at[total - 1], stage)
            white_copy = pltpu.make_async_copy(pair.at[total - 1], white, raw_sems.at[len(extras)])
            white_copy.start()
            lax.fori_loop(0, halves, each_raw_half, 0)
        table_copy.wait()
        if prior:
            prior_copy.wait()
        copies = []
        for begin in range(0, shape[0], chunk):
            size = min(chunk, shape[0] - begin)
            span = pl.ds(8 * begin, 8 * size)
            value = jnp.concatenate([lhs[half, span, :] for half in range(halves)], axis=1)
            lagged = dot_split(value, table_ref).reshape(size, 8, LAGS)
            place = pl.ds(begin, size)
            result[place] = result[place] + lagged if prior else lagged
            copies.append(pltpu.make_async_copy(result.at[place], out.at[place], out_sems.at[len(copies)]))
            copies[-1].start()
        for done in copies:
            done.wait()
        if raw is not None:
            white_copy.wait()

    far_memory = pl.BlockSpec(memory_space=pltpu.HBM)
    chunks = -(-shape[0] // chunk)
    results, spare = [jax.ShapeDtypeStruct(shape, jnp.float32)], []
    if raw is not None:
        results.append(jax.ShapeDtypeStruct(sample.shape, jnp.float32))
        spare = [pltpu.VMEM((raw.shape[2] // LANES, near * segs + segs, LANES), jnp.float32)]
        spare += [pltpu.VMEM(value.shape, value.dtype) for value in extras]
        spare.append(pltpu.SemaphoreType.DMA((len(extras) + 1,)))
    outputs = pl.pallas_call(
        kernel,
        in_specs=[far_memory] * (len(operands) + 1 + len(prior) + len(after) + len(extras)),
        out_specs=[far_memory] * len(results),
        out_shape=results,
        scratch_shapes=[
            pltpu.VMEM((total, halves, parts, segs, sides * near, lanes), jnp.float32),
            pltpu.VMEM((halves, rows, 2 * lanes), jnp.float32),
            pltpu.VMEM(table.shape, table.dtype),
            pltpu.VMEM(shape, jnp.float32),
            pltpu.SemaphoreType.DMA((len(sources), halves, 2)),
            pltpu.SemaphoreType.DMA,
            pltpu.SemaphoreType.DMA,
            pltpu.SemaphoreType.DMA((chunks,)),
        ]
        + spare,
        compiler_params=pltpu.CompilerParams(vmem_limit_bytes=VMEM_LIMIT),
        cost_estimate=pl.CostEstimate(flops=cost, bytes_accessed=1000, transcendentals=0),
        name="lag_" + which,
    )(*operands, table, *prior, *after, *extras)
    return outputs[0] if raw is None else outputs


def place(near, inside, across):
    count = len(inside)
    terms = [[term if isinstance(term, list) else [term] for term in kind] for kind in (inside, across)]
    operands = [value for kind in terms for term in kind for value, _ in term]
    kinds = ("inside", "across")
    parts = LAGS // LANES
    tiles = near // 8

    def kernel(*refs):
        given, refs = list(refs[: len(operands)]), refs[len(operands) :]
        sources = [[[(given.pop(0), begin) for _, begin in term] for term in kind] for kind in terms]
        out, buffers, (stage, in_sems, out_sems) = refs[0], refs[1:3], refs[3:]
        z = lax.axis_index("tm")
        end = (z == 0) | (z == 3)
        loads, groups = {}, {}
        for tile in range(tiles):
            for kind in range(2):
                known = groups_of(near, kinds[kind])
                mine = [index for index, group in enumerate(known) if group[0] == tile]
                groups[tile, kind] = [(index, known[index][1]) for index in mine]
                if not mine:
                    continue
                span = pl.ds(mine[0], len(mine))
                for term in range(count):
                    copies = [
                        pltpu.make_async_copy(
                            value.at[pl.ds(begin + mine[0], len(mine))],
                            buffers[kind].at[term, span],
                            in_sems.at[tile, kind, term],
                        )
                        for value, begin in sources[kind][term]
                    ]
                    loads[tile, kind, term] = copies[0]
                    if len(copies) == 1:
                        copies[0].start()
                    else:
                        pl.when(end)(copies[0].start)
                        pl.when(jnp.logical_not(end))(copies[1].start)
        stores = []
        for tile in range(tiles):
            for kind in range(2):
                for term in range(count):
                    if (tile, kind, term) in loads:
                        loads[tile, kind, term].wait()
                for index, offset in groups[tile, kind]:
                    value = buffers[kind][0, index]
                    for term in range(1, count):
                        value = value + buffers[kind][term, index]
                    for part in range(parts):
                        stage[part, pl.ds(8 * tile * near + offset - 1, 8, stride=near), :] = value[
                            :, LANES * part : LANES * part + LANES
                        ]
            for part in range(parts):
                stores.append(
                    pltpu.make_async_copy(
                        stage.at[part].reshape(near + 1, near, LANES).at[pl.ds(8 * tile, 8)],
                        out.at[pl.ds(8 * tile, 8), :, pl.ds(LANES * part, LANES)],
                        out_sems.at[tile, part],
                    )
                )
                stores[-1].start()
        for store in stores:
            store.wait()

    far_memory = pl.BlockSpec(memory_space=pltpu.HBM)
    return pl.pallas_call(
        kernel,
        in_specs=[far_memory] * len(operands),
        out_specs=far_memory,
        out_shape=jax.ShapeDtypeStruct((near, near, LAGS), jnp.float32),
        scratch_shapes=[pltpu.VMEM((count, len(groups_of(near, kind)), 8, LAGS), jnp.float32) for kind in kinds]
        + [
            pltpu.VMEM((parts, near * near + near, LANES), jnp.float32),
            pltpu.SemaphoreType.DMA((tiles, 2, count)),
            pltpu.SemaphoreType.DMA((tiles, parts)),
        ],
        compiler_params=pltpu.CompilerParams(vmem_limit_bytes=VMEM_LIMIT),
        cost_estimate=pl.CostEstimate(flops=COST, bytes_accessed=1000, transcendentals=0),
        name="place",
    )(*operands)


def shifted(value, steps):
    count = lax.axis_size("fibre")
    return lax.ppermute(value, "fibre", [(source, source + steps) for source in range(max(0, -steps), count)])


def line_of_four(traces):
    channels, segs, win = traces.shape
    tables = make_tables(win, LAGS, segs * 4)
    blocks = traces.reshape(4, NEAR, segs, win)
    fibres = lax.axis_size("fibre")

    def outer(value):
        return lax.ppermute(value, "tm", [(0, 1), (3, 2)])

    def outer_next(value):
        pairs = [(4 * fibre + 4, 4 * fibre + 1) for fibre in range(fibres - 1)]
        pairs += [(4 * fibre + 3, 4 * fibre + 2) for fibre in range(fibres)]
        return lax.ppermute(value, ("fibre", "tm"), pairs)

    def middle(value):
        return lax.ppermute(value, "tm", [(1, 2), (2, 1)])

    def inner(value):
        return lax.ppermute(value, "tm", [(1, 0), (2, 3)])

    far = take_far(blocks)
    e1 = outer(far)
    *own, next_far, last = whiten_own(blocks, tables, far)
    e2 = outer_next(next_far)
    own.append(shifted(own[0], -1))
    e3 = outer(own[2])

    role = lambda z: jnp.where(z < 2, 0, 1)
    jobs = functools.partial(lag_sums, tables=tables, inner=True)
    back_in = jobs("inside", [([own[0], own[3]], None)], role=role, cost=1_000_000)
    m1, e1 = jobs("inside", [([own[3], own[0]], None)], role=role, after=[back_in], raw=e1)
    m1_in = middle(m1)
    base = jobs("across", [([own[3], own[0]], [own[4], own[1]])], role=role, after=[m1])
    m2 = jobs("across", [([e1], [e2])], prior=[base])
    m2_in = middle(m2)
    m1_in, _ = lax.optimization_barrier((m1_in, m2))
    first = m1_in + back_in
    i1 = inner(first)
    last, _ = lax.optimization_barrier((last, first))
    e4 = outer(last)
    m3 = jobs("all", [([own[2], own[1]], [own[3], own[2]]), ([e3, e2], [e1, e3])], role=role, after=[first])
    m3_in = middle(m3)
    second = jobs("across", [([own[0], own[3]], [own[1], own[4]])], role=role, prior=[m2_in], after=[m3])
    i2 = inner(second)
    near = lag_sums(
        "all", [(own[:4], own[1:]), ([e4, e4, e3, e4], [e3, e3, e4, e3])], tables, lambda z: z, after=[second]
    )
    start = m1.shape[0]
    return place(NEAR, [(near, 0), [(i1, 0), (m3_in, 0)]], [(near, start), [(i2, 0), (m3_in, start)]])


def any_line(traces):
    channels, segs, win = traces.shape
    tables = make_tables(win, LAGS, segs * lax.axis_size("tm"))
    count = channels // NEAR
    blocks = traces.reshape(count, NEAR, segs, win)
    halo = shifted(blocks[0], -1)
    spectra = whiten(blocks, tables, count) + whiten(halo[None], tables, 1)
    start = len(groups_of(NEAR, "inside"))
    pieces = []
    for index in range(count):
        sums = lag_sums("all", [([spectra[index]], [spectra[index + 1]])], tables)
        pieces.append(place(NEAR, [(sums, 0)], [(sums, start)]))
    return lax.psum_scatter(jnp.concatenate(pieces, axis=0), "tm", scatter_dimension=0, tiled=True)


def shards(traces):
    if lax.axis_size("tm") == 4 and traces.shape[0] == 4 * NEAR:
        return line_of_four(traces)
    return any_line(traces)


def solution(mesh):
    in_specs = (P("fibre", "tm", None),)
    out_specs = P(("fibre", "tm"), None, None)
    return jax.shard_map(shards, mesh=mesh, in_specs=in_specs, out_specs=out_specs, check_vma=False)
```

```python
import functools

import jax
import jax.numpy as jnp
import ml_dtypes
import numpy as np
from jax import lax
from jax.experimental import pallas as pl
from jax.experimental.pallas import tpu as pltpu
from jax.sharding import PartitionSpec as P

NEAR = 32
LAGS = 256
HALF = 8
LANES = 128
VMEM_LIMIT = 64 << 20
COST = 10_000_000_000


def split_table(table):
    high = table.astype(ml_dtypes.bfloat16)
    low = (table - high.astype(np.float64)).astype(ml_dtypes.bfloat16)
    return np.concatenate([high, low], axis=0)


def make_tables(win, lags, segs):
    bins = win // 2
    samples = np.arange(win)
    hann = 0.5 - 0.5 * np.cos(2.0 * np.pi * samples / win)
    even, odd = np.arange(2, bins + 1, 2), np.arange(1, bins, 2)
    order = np.concatenate([even, odd])

    def forward(picked):
        phases = 2.0 * np.pi * ((samples[: win // 2, None] * picked[None, :]) % win) / win
        return split_table(np.concatenate([np.cos(phases), -np.sin(phases)], axis=1))

    near = np.abs(order[:, None] - order[None, :]) <= HALF
    band = near / (2.0 * HALF + 1.0) + 0.1 / bins
    lag = np.arange(lags) - lags // 2
    phases = 2.0 * np.pi * ((order[:, None] * lag[None, :]) % win) / win
    rows = [part for half in np.split(phases, 2) for part in (np.cos(half), -np.sin(half))]
    return {
        "hann": np.tile(hann.astype(np.float32)[None, :], (8, 1)),
        "forward": np.stack([forward(even), forward(odd), split_table(band)]),
        "inverse": split_table(np.concatenate(rows, axis=0) / segs),
    }


def dot_split(value, table):
    high = value.astype(jnp.bfloat16)
    low = (value - high.astype(jnp.float32)).astype(jnp.bfloat16)
    dot = functools.partial(jnp.dot, preferred_element_type=jnp.float32)
    return dot(jnp.concatenate([high, high], axis=1), table[...]) + dot(low, table[: value.shape[1]])


def whiten_block(x_ref, hann, forward, w_ref, stage):
    channels, segs, win = x_ref.shape
    parts = win // LANES
    for part in range(parts):
        lanes = slice(LANES * part, LANES * part + LANES)
        stage[part, pl.ds(0, channels * segs)] = x_ref[:, :, lanes].reshape(channels * segs, LANES)
    pieces = []
    for s in range(segs):
        pieces.append([
            stage[part, pl.ds(s, channels, stride=segs), :] * hann[0:1, LANES * part : LANES * part + LANES]
            for part in range(parts)
        ])
    quarter = [jnp.concatenate([piece[part] for piece in pieces], axis=0) for part in range(parts)]
    both = jnp.concatenate([quarter[0] + quarter[2], quarter[1] + quarter[3]], axis=1)
    between = jnp.concatenate([quarter[0] - quarter[2], quarter[1] - quarter[3]], axis=1)
    spectra = (dot_split(both, forward.at[0]), dot_split(between, forward.at[1]))
    energy = jnp.concatenate(
        [sp[:, :LANES] * sp[:, :LANES] + sp[:, LANES:] * sp[:, LANES:] for sp in spectra], axis=1
    )
    scale = lax.rsqrt(dot_split(energy, forward.at[2]) + 1e-06)
    for half, sp in enumerate(spectra):
        own = scale[:, LANES * half : LANES * half + LANES]
        real, imag = sp[:, :LANES] * own, sp[:, LANES:] * own
        for s in range(segs):
            rows = slice(channels * s, channels * s + channels)
            w_ref[half, 0, s] = real[rows]
            w_ref[half, 1, s] = imag[rows]


def whiten(x, tables, count):
    near, segs, win = x.shape[1:]
    consts = [jnp.asarray(tables["hann"]), jnp.asarray(tables["forward"])]

    def kernel(*refs):
        x_any, hann_any, forward_any = refs[:3]
        outs, refs = refs[3 : 3 + count], refs[3 + count :]
        stage, hann, forward, blocks_in, blocks_out, sems, out_sems = refs
        loads = [pltpu.make_async_copy(x_any.at[b], blocks_in.at[b], sems.at[b]) for b in range(count)]
        tabs = [
            pltpu.make_async_copy(hann_any, hann, sems.at[count]),
            pltpu.make_async_copy(forward_any, forward, sems.at[count + 1]),
        ]
        for load in tabs + loads:
            load.start()
        for load in tabs:
            load.wait()
        stores = []
        for index in range(count):
            loads[index].wait()
            whiten_block(blocks_in.at[index], hann, forward, blocks_out.at[index], stage)
            stores.append(pltpu.make_async_copy(blocks_out.at[index], outs[index], out_sems.at[index]))
            stores[-1].start()
        for store in stores:
            store.wait()

    shape = (2, 2, segs, near, LANES)
    far_memory = pl.BlockSpec(memory_space=pltpu.HBM)
    return pl.pallas_call(
        kernel,
        in_specs=[far_memory] * 3,
        out_specs=[far_memory] * count,
        out_shape=[jax.ShapeDtypeStruct(shape, jnp.float32)] * count,
        scratch_shapes=[
            pltpu.VMEM((win // LANES, near * segs + segs, LANES), jnp.float32),
            pltpu.VMEM(consts[0].shape, consts[0].dtype),
            pltpu.VMEM(consts[1].shape, consts[1].dtype),
            pltpu.VMEM((count, near, segs, win), jnp.float32),
            pltpu.VMEM((count,) + shape, jnp.float32),
            pltpu.SemaphoreType.DMA((count + 2,)),
            pltpu.SemaphoreType.DMA((count,)),
        ],
        compiler_params=pltpu.CompilerParams(vmem_limit_bytes=VMEM_LIMIT),
        cost_estimate=pl.CostEstimate(flops=COST, bytes_accessed=1000, transcendentals=0),
        name="whiten",
    )(x, *consts)


def take_far(x):
    chunks = 4
    step = x.shape[1] // chunks

    def kernel(x_any, out, held, in_sems, out_sems):
        z = lax.axis_index("tm")

        @pl.when((z == 0) | (z == 3))
        def _():
            place = jnp.where(z < 2, 3, 0)
            spans = [pl.ds(step * chunk, step) for chunk in range(chunks)]
            loads = [
                pltpu.make_async_copy(x_any.at[place, span], held.at[span], in_sems.at[chunk])
                for chunk, span in enumerate(spans)
            ]
            stores = [
                pltpu.make_async_copy(held.at[span], out.at[span], out_sems.at[chunk])
                for chunk, span in enumerate(spans)
            ]
            for load in loads:
                load.start()
            for load, store in zip(loads, stores):
                load.wait()
                store.start()
            for store in stores:
                store.wait()

    far_memory = pl.BlockSpec(memory_space=pltpu.HBM)
    return pl.pallas_call(
        kernel,
        in_specs=[far_memory],
        out_specs=far_memory,
        out_shape=jax.ShapeDtypeStruct(x.shape[1:], jnp.float32),
        scratch_shapes=[
            pltpu.VMEM(x.shape[1:], jnp.float32),
            pltpu.SemaphoreType.DMA((chunks,)),
            pltpu.SemaphoreType.DMA((chunks,)),
        ],
        compiler_params=pltpu.CompilerParams(vmem_limit_bytes=VMEM_LIMIT),
        cost_estimate=pl.CostEstimate(flops=COST, bytes_accessed=1000, transcendentals=0),
        name="take_far",
    )(x)


def whiten_own(x, tables, after):
    near, segs, win = x.shape[1:]
    consts = [jnp.asarray(tables["hann"]), jnp.asarray(tables["forward"])]
    copies = ((0, 1), (1, 3))

    def kernel(x_any, hann_any, forward_any, _, *refs):
        outs, (stage, hann, forward, blocks_in, blocks_out, sems, out_sems) = refs[:6], refs[6:]
        z = lax.axis_index("tm")
        loads = [pltpu.make_async_copy(x_any.at[b], blocks_in.at[b], sems.at[b]) for b in range(4)]
        tabs = [
            pltpu.make_async_copy(hann_any, hann, sems.at[4]),
            pltpu.make_async_copy(forward_any, forward, sems.at[5]),
        ]
        for load in loads[:1] + tabs + loads[1:]:
            load.start()
        for tab in tabs:
            tab.wait()
        stores = []
        for b in range(4):
            loads[b].wait()
            whiten_block(blocks_in.at[b], hann, forward, blocks_out.at[b], stage)
            stores.append(pltpu.make_async_copy(blocks_out.at[b], outs[b], out_sems.at[b]))
            stores[-1].start()
        for at, sources in enumerate(copies):
            for side, source in enumerate(sources):

                @pl.when(z < 2 if side == 0 else z >= 2)
                def _():
                    pltpu.make_async_copy(blocks_out.at[source], outs[4 + at], out_sems.at[4 + at]).start()

            stores.append(pltpu.make_async_copy(blocks_out.at[sources[0]], outs[4 + at], out_sems.at[4 + at]))
        for store in stores:
            store.wait()

    shape = (2, 2, segs, near, LANES)
    far_memory = pl.BlockSpec(memory_space=pltpu.HBM)
    return pl.pallas_call(
        kernel,
        in_specs=[far_memory] * 4,
        out_specs=[far_memory] * 6,
        out_shape=[jax.ShapeDtypeStruct(shape, jnp.float32)] * 6,
        scratch_shapes=[
            pltpu.VMEM((win // LANES, near * segs + segs, LANES), jnp.float32),
            pltpu.VMEM(consts[0].shape, consts[0].dtype),
            pltpu.VMEM(consts[1].shape, consts[1].dtype),
            pltpu.VMEM((4, near, segs, win), jnp.float32),
            pltpu.VMEM((4,) + shape, jnp.float32),
            pltpu.SemaphoreType.DMA((6,)),
            pltpu.SemaphoreType.DMA((6,)),
        ],
        compiler_params=pltpu.CompilerParams(vmem_limit_bytes=VMEM_LIMIT),
        cost_estimate=pl.CostEstimate(flops=COST, bytes_accessed=1000, transcendentals=0),
        name="whiten_own",
    )(x, *consts, after)


def groups_of(near, which):
    tiles = near // 8
    inside = [(tile, offset) for tile in range(tiles) for offset in range(1, near - 8 * tile - 7)]
    across = [(tile, offset) for tile in range(tiles) for offset in range(near - 8 * tile - 7, near + 1)]
    return {"inside": inside, "across": across, "all": inside + across}[which]


def products(pair, half, lhs, groups, fresh, batch=4):
    segs = pair.shape[2]
    index_of = {group: index for index, group in enumerate(groups)}
    tiles = sorted({tile for tile, _ in groups})
    for begin in range(0, segs, batch):
        span = range(begin, min(begin + batch, segs))
        real = {t: [pair[half, 0, s, pl.ds(8 * t, 8), :] for s in span] for t in tiles}
        imag = {t: [pair[half, 1, s, pl.ds(8 * t, 8), :] for s in span] for t in tiles}
        added = {t: [re + im for re, im in zip(real[t], imag[t])] for t in tiles}
        for row in range(1, 8 * len(tiles) + NEAR):
            units = [(t, row - 8 * t) for t in tiles if (t, row - 8 * t) in index_of]
            if not units:
                continue
            sums = {}
            for at, s in enumerate(span):
                other_re = pair[half, 0, s, pl.ds(row, 8), :]
                other_im = pair[half, 1, s, pl.ds(row, 8), :]
                apart = other_re - other_im
                for unit in units:
                    t = unit[0]
                    terms = (real[t][at] * other_re, imag[t][at] * other_im, added[t][at] * apart)
                    sums[unit] = terms if at == 0 else tuple(old + new for old, new in zip(sums[unit], terms))
            for unit in units:
                rr, ii, mixed = sums[unit]
                cross_re, cross_im = rr + ii, mixed - rr + ii
                rows = pl.ds(8 * index_of[unit], 8)
                if not (fresh and begin == 0):
                    cross_re = cross_re + lhs[half, rows, :LANES]
                    cross_im = cross_im + lhs[half, rows, LANES:]
                lhs[half, rows, :LANES] = cross_re
                lhs[half, rows, LANES:] = cross_im


def lag_sums(which, sources, tables, role=None, prior=(), after=(), cost=COST, inner=False, raw=None):
    table = jnp.asarray(tables["inverse"])
    sample = sources[0][0][0]
    halves, parts, segs, near, lanes = sample.shape
    groups = groups_of(near, which)
    sides = 1 if which == "inside" else 2
    operands, layout = [], []
    for source in sources:
        layout.append([])
        for side in range(sides):
            places = []
            for value in source[side]:
                known = [i for i, other in enumerate(operands) if other is value]
                if not known:
                    operands.append(value)
                places.append(known[0] if known else len(operands) - 1)
            layout[-1].append(places)
    shape = (len(groups), 8, LAGS)
    total = len(sources) + (raw is not None)
    extras = [] if raw is None else [raw, jnp.asarray(tables["hann"]), jnp.asarray(tables["forward"])]
    rows = 8 * len(groups)
    chunk = 16

    def kernel(*refs):
        if not inner:
            return work(*refs)
        z = lax.axis_index("tm")
        pl.when((z == 1) | (z == 2))(lambda: work(*refs))

    def work(*refs):
        cands, table_any = refs[: len(operands)], refs[len(operands)]
        refs = refs[len(operands) + 1 :]
        priors, refs = refs[: len(prior)], refs[len(prior) + len(after) :]
        samples, refs = refs[: len(extras)], refs[len(extras) :]
        out, refs = refs[0], refs[1:]
        if raw is not None:
            white, refs = refs[0], refs[1:]
        pair, lhs, table_ref, result, in_sems, table_sem, prior_sem, out_sems = refs[:8]
        if raw is not None:
            stage, raw_sems = refs[8], refs[-1]
            held = refs[9:-1]
            raw_copies = [
                pltpu.make_async_copy(source, place, raw_sems.at[index])
                for index, (source, place) in enumerate(zip(samples, held))
            ]
        pick = role(lax.axis_index("tm")) if role is not None else None

        def copy(number, side, half, place):
            return pltpu.make_async_copy(
                cands[place].at[half],
                pair.at[number, half, :, :, pl.ds(side * near, near), :],
                in_sems.at[number, half, side],
            )

        if raw is not None:
            for raw_copy in raw_copies:
                raw_copy.start()
        for half in range(halves):
            for number, source in enumerate(layout):
                for side, places in enumerate(source):
                    if len(places) == 1:
                        copy(number, side, half, places[0]).start()
                        continue
                    for choice, place in enumerate(places):

                        @pl.when(pick == choice)
                        def _():
                            copy(number, side, half, place).start()

        table_copy = pltpu.make_async_copy(table_any, table_ref, table_sem)
        table_copy.start()
        if prior:
            prior_copy = pltpu.make_async_copy(priors[0], result, prior_sem)
            prior_copy.start()

        def each_half(half, _):
            for number, source in enumerate(layout):
                for side, places in enumerate(source):
                    copy(number, side, half, places[0]).wait()
                products(pair.at[number], half, lhs, groups, number == 0)
            return 0

        def each_raw_half(half, _):
            products(pair.at[total - 1], half, lhs, groups, False)
            return 0

        lax.fori_loop(0, halves, each_half, 0)
        if raw is not None:
            for raw_copy in raw_copies:
                raw_copy.wait()
            whiten_block(held[0], held[1], held[2], pair.at[total - 1], stage)
            white_copy = pltpu.make_async_copy(pair.at[total - 1], white, raw_sems.at[len(extras)])
            white_copy.start()
            lax.fori_loop(0, halves, each_raw_half, 0)
        table_copy.wait()
        if prior:
            prior_copy.wait()
        copies = []
        for begin in range(0, shape[0], chunk):
            size = min(chunk, shape[0] - begin)
            span = pl.ds(8 * begin, 8 * size)
            value = jnp.concatenate([lhs[half, span, :] for half in range(halves)], axis=1)
            lagged = dot_split(value, table_ref).reshape(size, 8, LAGS)
            place = pl.ds(begin, size)
            result[place] = result[place] + lagged if prior else lagged
            copies.append(pltpu.make_async_copy(result.at[place], out.at[place], out_sems.at[len(copies)]))
            copies[-1].start()
        for done in copies:
            done.wait()
        if raw is not None:
            white_copy.wait()

    far_memory = pl.BlockSpec(memory_space=pltpu.HBM)
    chunks = -(-shape[0] // chunk)
    results, spare = [jax.ShapeDtypeStruct(shape, jnp.float32)], []
    if raw is not None:
        results.append(jax.ShapeDtypeStruct(sample.shape, jnp.float32))
        spare = [pltpu.VMEM((raw.shape[2] // LANES, near * segs + segs, LANES), jnp.float32)]
        spare += [pltpu.VMEM(value.shape, value.dtype) for value in extras]
        spare.append(pltpu.SemaphoreType.DMA((len(extras) + 1,)))
    outputs = pl.pallas_call(
        kernel,
        in_specs=[far_memory] * (len(operands) + 1 + len(prior) + len(after) + len(extras)),
        out_specs=[far_memory] * len(results),
        out_shape=results,
        scratch_shapes=[
            pltpu.VMEM((total, halves, parts, segs, sides * near, lanes), jnp.float32),
            pltpu.VMEM((halves, rows, 2 * lanes), jnp.float32),
            pltpu.VMEM(table.shape, table.dtype),
            pltpu.VMEM(shape, jnp.float32),
            pltpu.SemaphoreType.DMA((len(sources), halves, 2)),
            pltpu.SemaphoreType.DMA,
            pltpu.SemaphoreType.DMA,
            pltpu.SemaphoreType.DMA((chunks,)),
        ]
        + spare,
        compiler_params=pltpu.CompilerParams(vmem_limit_bytes=VMEM_LIMIT),
        cost_estimate=pl.CostEstimate(flops=cost, bytes_accessed=1000, transcendentals=0),
        name="lag_" + which,
    )(*operands, table, *prior, *after, *extras)
    return outputs[0] if raw is None else outputs


def place(near, inside, across):
    count = len(inside)
    terms = [[term if isinstance(term, list) else [term] for term in kind] for kind in (inside, across)]
    operands = [value for kind in terms for term in kind for value, _ in term]
    kinds = ("inside", "across")
    parts = LAGS // LANES
    tiles = near // 8

    def kernel(*refs):
        given, refs = list(refs[: len(operands)]), refs[len(operands) :]
        sources = [[[(given.pop(0), begin) for _, begin in term] for term in kind] for kind in terms]
        out, buffers, (stage, in_sems, out_sems) = refs[0], refs[1:3], refs[3:]
        z = lax.axis_index("tm")
        end = (z == 0) | (z == 3)
        loads, groups = {}, {}
        for tile in range(tiles):
            for kind in range(2):
                known = groups_of(near, kinds[kind])
                mine = [index for index, group in enumerate(known) if group[0] == tile]
                groups[tile, kind] = [(index, known[index][1]) for index in mine]
                if not mine:
                    continue
                span = pl.ds(mine[0], len(mine))
                for term in range(count):
                    copies = [
                        pltpu.make_async_copy(
                            value.at[pl.ds(begin + mine[0], len(mine))],
                            buffers[kind].at[term, span],
                            in_sems.at[tile, kind, term],
                        )
                        for value, begin in sources[kind][term]
                    ]
                    loads[tile, kind, term] = copies[0]
                    if len(copies) == 1:
                        copies[0].start()
                    else:
                        pl.when(end)(copies[0].start)
                        pl.when(jnp.logical_not(end))(copies[1].start)
        stores = []
        for tile in range(tiles):
            for kind in range(2):
                for term in range(count):
                    if (tile, kind, term) in loads:
                        loads[tile, kind, term].wait()
                for index, offset in groups[tile, kind]:
                    value = buffers[kind][0, index]
                    for term in range(1, count):
                        value = value + buffers[kind][term, index]
                    for part in range(parts):
                        stage[part, pl.ds(8 * tile * near + offset - 1, 8, stride=near), :] = value[
                            :, LANES * part : LANES * part + LANES
                        ]
            for part in range(parts):
                stores.append(
                    pltpu.make_async_copy(
                        stage.at[part].reshape(near + 1, near, LANES).at[pl.ds(8 * tile, 8)],
                        out.at[pl.ds(8 * tile, 8), :, pl.ds(LANES * part, LANES)],
                        out_sems.at[tile, part],
                    )
                )
                stores[-1].start()
        for store in stores:
            store.wait()

    far_memory = pl.BlockSpec(memory_space=pltpu.HBM)
    return pl.pallas_call(
        kernel,
        in_specs=[far_memory] * len(operands),
        out_specs=far_memory,
        out_shape=jax.ShapeDtypeStruct((near, near, LAGS), jnp.float32),
        scratch_shapes=[pltpu.VMEM((count, len(groups_of(near, kind)), 8, LAGS), jnp.float32) for kind in kinds]
        + [
            pltpu.VMEM((parts, near * near + near, LANES), jnp.float32),
            pltpu.SemaphoreType.DMA((tiles, 2, count)),
            pltpu.SemaphoreType.DMA((tiles, parts)),
        ],
        compiler_params=pltpu.CompilerParams(vmem_limit_bytes=VMEM_LIMIT),
        cost_estimate=pl.CostEstimate(flops=COST, bytes_accessed=1000, transcendentals=0),
        name="place",
    )(*operands)


def shifted(value, steps):
    count = lax.axis_size("fibre")
    return lax.ppermute(value, "fibre", [(source, source + steps) for source in range(max(0, -steps), count)])


def line_of_four(traces):
    channels, segs, win = traces.shape
    tables = make_tables(win, LAGS, segs * 4)
    blocks = traces.reshape(4, NEAR, segs, win)
    fibres = lax.axis_size("fibre")

    def outer(value):
        return lax.ppermute(value, "tm", [(0, 1), (3, 2)])

    def outer_next(value):
        pairs = [(4 * fibre + 4, 4 * fibre + 1) for fibre in range(fibres - 1)]
        pairs += [(4 * fibre + 3, 4 * fibre + 2) for fibre in range(fibres)]
        return lax.ppermute(value, ("fibre", "tm"), pairs)

    def middle(value):
        return lax.ppermute(value, "tm", [(1, 2), (2, 1)])

    def inner(value):
        return lax.ppermute(value, "tm", [(1, 0), (2, 3)])

    far = take_far(blocks)
    e1 = outer(far)
    *own, next_far, last = whiten_own(blocks, tables, far)
    e2 = outer_next(next_far)
    own.append(shifted(own[0], -1))
    e3 = outer(own[2])

    role = lambda z: jnp.where(z < 2, 0, 1)
    jobs = functools.partial(lag_sums, tables=tables, inner=True)
    back_in = jobs("inside", [([own[0], own[3]], None)], role=role, cost=1_000_000)
    m1, e1 = jobs("inside", [([own[3], own[0]], None)], role=role, after=[back_in], raw=e1)
    m1_in = middle(m1)
    base = jobs("across", [([own[3], own[0]], [own[4], own[1]])], role=role, after=[m1])
    m2 = jobs("across", [([e1], [e2])], prior=[base])
    m2_in = middle(m2)
    m1_in, _ = lax.optimization_barrier((m1_in, m2))
    first = m1_in + back_in
    i1 = inner(first)
    last, _ = lax.optimization_barrier((last, first))
    e4 = outer(last)
    m3 = jobs("all", [([own[2], own[1]], [own[3], own[2]]), ([e3, e2], [e1, e3])], role=role, after=[first])
    m3_in = middle(m3)
    second = jobs("across", [([own[0], own[3]], [own[1], own[4]])], role=role, prior=[m2_in], after=[m3])
    i2 = inner(second)
    near = lag_sums(
        "all", [(own[:4], own[1:]), ([e4, e4, e3, e4], [e3, e3, e4, e3])], tables, lambda z: z, after=[second]
    )
    start = m1.shape[0]
    return place(NEAR, [(near, 0), [(i1, 0), (m3_in, 0)]], [(near, start), [(i2, 0), (m3_in, start)]])


def any_line(traces):
    channels, segs, win = traces.shape
    tables = make_tables(win, LAGS, segs * lax.axis_size("tm"))
    count = channels // NEAR
    blocks = traces.reshape(count, NEAR, segs, win)
    halo = shifted(blocks[0], -1)
    spectra = whiten(blocks, tables, count) + whiten(halo[None], tables, 1)
    start = len(groups_of(NEAR, "inside"))
    pieces = []
    for index in range(count):
        sums = lag_sums("all", [([spectra[index]], [spectra[index + 1]])], tables)
        pieces.append(place(NEAR, [(sums, 0)], [(sums, start)]))
    return lax.psum_scatter(jnp.concatenate(pieces, axis=0), "tm", scatter_dimension=0, tiled=True)


def shards(traces):
    if lax.axis_size("tm") == 4 and traces.shape[0] == 4 * NEAR:
        return line_of_four(traces)
    return any_line(traces)


def solution(mesh):
    in_specs = (P("fibre", "tm", None),)
    out_specs = P(("fibre", "tm"), None, None)
    return jax.shard_map(shards, mesh=mesh, in_specs=in_specs, out_specs=out_specs, check_vma=False)
```
